32 devices in a mesh: row: 4 (over y, core), col: 8 (over z, x).
Axes of the slice: x: 2, y: 2, z: 4, core: 2. Of those that a mesh axis runs over, the one named last changes fastest.
Arguments:
- objects: float32 [2, 2, 1024, 2048], P(None, None, 'row', 'col'), may hold values from -5 to 5
- probe: float32 [2, 2, 128, 128], replicated, may hold values from -6 to 6
- amplitudes: bfloat16 [4, 8, 6, 128, 128], P('row', 'col'), may hold values from 0.29882812 to 3
- owners: int32 [4, 8, 6], P('row', 'col'), may hold values from 0 to 7, as said below
- off_rows: int32 [4, 8, 6], P('row', 'col'), may hold values from 0 to 256
- off_cols: int32 [4, 8, 6], P('row', 'col'), may hold values from 0 to 256
Outputs:
- gradient: float32 [2, 2, 1024, 2048], P(None, None, 'row', 'col')
The draws below stay inside these ranges and needn't reach their ends.
Inputs may be any that keep to these rules, and one draw needn't show every extreme that they name: Each device's 6 positions go to owners of its own tile row whose tile column is the device's own plus one of -3, -2, -1, 1, 2, 3, 4, taken modulo 8; at most 2 of them to one owner, exactly 2 to one owner from some device of every tile row. Over all devices of a tile row, one owner receives exactly 12 positions and every other owner at most 7.
All inputs are finite; a program needn't handle non-finite values.
Results may differ from the reference program's by a relative error of at most 0.009.
Values may be sent and summed in bfloat16 or wider, within the bound.
No kernel may reach another device: no remote copies, remote signals or barrier semaphores. Data moves between devices by JAX's collectives and lax.ppermute only.
A program may use at most 64 MiB of HBM per device.

```python
import math
import jax
import jax.numpy as jnp
from jax import lax

P_SIZE = 128
MODES = 2
SLICES = 2
SRC_DEV = 6
TH = 256
TW = 256
B = 64
GRID_R = 4
GRID_C = 8
OH = 1024
OW = 2048


REACH_OFFSETS = (-3, -2, -1, 1, 2, 3, 4)


def draw_owners(key, part):
    keys = jax.random.split(key, GRID_R)
    reach = jnp.array(REACH_OFFSETS, dtype=jnp.int32)
    kinds = reach.shape[0]

    def one_row(row_key):
        first, second, third, fourth = jax.random.split(row_key, 4)
        hottest = jax.random.randint(first, (), 0, GRID_C, dtype=jnp.int32)
        hot_order = jax.random.permutation(second, kinds).astype(jnp.int32)
        cold_kind = hot_order[kinds - 1]
        sources = jnp.arange(GRID_C, dtype=jnp.int32)
        apart = (hottest - sources) % GRID_C
        match = apart[:, None] == reach[None, :] % GRID_C
        kind_ids = jnp.arange(kinds, dtype=jnp.int32)
        is_cold = kind_ids[None, :] == cold_kind
        hot_match = match & jnp.logical_not(is_cold)
        cold_match = match & is_cold
        hot_source = jnp.any(hot_match, axis=1)
        raw = jax.random.randint(third, (GRID_C, kinds), 0, 1000, dtype=jnp.int32)
        scores = raw * 8 + kind_ids[None, :]
        scores = jnp.where(hot_match, -1, jnp.where(cold_match, 100000, scores))
        order = jnp.argsort(scores, axis=1, stable=True)[:, :SRC_DEV]
        base = (sources[:, None] + reach[order]) % GRID_C
        slot = jnp.arange(SRC_DEV, dtype=jnp.int32)
        moved = hot_source[:, None] & (slot[None, :] == 1)
        owners_row = jnp.where(moved, hottest, base).astype(jnp.int32)
        mix = jax.random.randint(fourth, (GRID_C, SRC_DEV), 0, 1000, dtype=jnp.int32)
        mix = mix * 8 + slot[None, :]
        shuffle = jnp.argsort(mix, axis=1, stable=True)
        return jnp.take_along_axis(owners_row, shuffle, axis=1).astype(jnp.int32)
    return jax.vmap(one_row)(keys)


def plant(result, own_key, low, top_value):
    longest = result.shape.index(max(result.shape))
    spots = []
    for shift in (0, 1):
        where = [jax.random.randint(jax.random.fold_in(own_key, axis), (), 0, length) for axis, length in enumerate(result.shape)]
        where[longest] = (where[longest] + shift) % result.shape[longest]
        spots.append(tuple(where))
    return result.at[spots[0]].set(low).at[spots[1]].set(top_value)


def steps_of(stream_key, shape, pieces, smallest, high):
    factor_of = 1.0
    for axis_at, parts in pieces:
        steps = jax.random.uniform(jax.random.fold_in(jax.random.fold_in(stream_key, 6), axis_at), (parts,), jnp.float32, smallest / len(pieces), high / len(pieces))
        factor_of = factor_of * jnp.repeat(jnp.exp(steps), shape[axis_at] // parts).reshape((-1,) + (1,) * (len(shape) - 1 - axis_at))
    return factor_of


def gaussian(rng, dims, scale, bound, cuts=(), kind=jnp.bfloat16):
    drawn = scale * jax.random.normal(rng, dims, jnp.float32)
    if cuts:
        drawn = drawn * steps_of(rng, dims, cuts, -0.22, 0.18)
    return jnp.clip(drawn, -bound, bound).astype(kind)


def setup_inputs(seed: int = 0) -> dict:
    key_list = jax.random.split(jax.random.key(seed), 7)
    return {
        "objects": gaussian(key_list[0], (SLICES, 2, OH, OW), 0.7, 5.0, ((2, 4), (3, 8)), jnp.float32),
        "probe": gaussian(key_list[1], (MODES, 2, P_SIZE, P_SIZE), 1.0, 6.0, (), jnp.float32),
        "amplitudes": jnp.clip(jnp.exp(math.log(3.0) - 2.306499 * jax.random.uniform(key_list[2], (GRID_R, GRID_C, SRC_DEV, P_SIZE, P_SIZE), jnp.float32) ** steps_of(key_list[2], (GRID_R, GRID_C, SRC_DEV, P_SIZE, P_SIZE), ((0, 4), (1, 8)), -0.2, 0.2)), 0.29882812, 3.0).astype(jnp.bfloat16),
        "owners": draw_owners(jax.random.fold_in(key_list[6], 71), 0),
        "off_rows": plant(jax.random.randint(key_list[4], (GRID_R, GRID_C, SRC_DEV), 0, TH + 2 * B - P_SIZE + 1), jax.random.fold_in(key_list[4], 1), 0, TH + 2 * B - P_SIZE).astype(jnp.int32),
        "off_cols": plant(jax.random.randint(key_list[5], (GRID_R, GRID_C, SRC_DEV), 0, TW + 2 * B - P_SIZE + 1), jax.random.fold_in(key_list[5], 1), 0, TW + 2 * B - P_SIZE).astype(jnp.int32),
    }


FRESNEL = 24.0

def make_mats(width):
    idx = jnp.arange(width, dtype=jnp.int32)
    prod = idx[:, None] * idx[None, :] % width
    angle = prod.astype(jnp.float32) * (2.0 * math.pi / width)
    scale = 1.0 / math.sqrt(width)
    f_re = jnp.cos(angle) * scale
    f_im = -jnp.sin(angle) * scale
    centred = (idx + width // 2) % width - width // 2
    theta = (centred * centred).astype(jnp.float32) * (math.pi * FRESNEL / (width * width))
    d_re = jnp.cos(theta)
    d_im = -jnp.sin(theta)
    m_re = d_re[:, None] * f_re - d_im[:, None] * f_im
    m_im = d_re[:, None] * f_im + d_im[:, None] * f_re
    high = lax.Precision.HIGHEST
    k_re = jnp.dot(f_re, m_re, precision=high) + jnp.dot(f_im, m_im, precision=high)
    k_im = jnp.dot(f_re, m_im, precision=high) - jnp.dot(f_im, m_re, precision=high)
    f_re = f_re.astype(jnp.bfloat16)
    f_im = f_im.astype(jnp.bfloat16)
    k_re = k_re.astype(jnp.bfloat16)
    k_im = k_im.astype(jnp.bfloat16)

    def left_stack(a_re, a_im):
        return jnp.stack([jnp.stack([a_re, -a_im]), jnp.stack([a_im, a_re])])

    def right_stack(a_re, a_im):
        return jnp.stack([jnp.stack([a_re, a_im]), jnp.stack([-a_im, a_re])])
    return (left_stack(k_re, k_im), right_stack(k_re, k_im), left_stack(f_re, f_im), right_stack(f_re, f_im), left_stack(k_re, -k_im), right_stack(k_re, -k_im), left_stack(f_re, -f_im), right_stack(f_re, -f_im))

def apply_left(table, field):
    return jnp.einsum('trpq,nrqs->ntps', table.astype(jnp.float32), field.astype(jnp.float32))

def apply_right(field, table):
    return jnp.einsum('nrpq,rtqs->ntps', field.astype(jnp.float32), table.astype(jnp.float32))

def cmul(first, second):
    a_re = first[..., 0, :, :]
    a_im = first[..., 1, :, :]
    b_re = second[..., 0, :, :]
    b_im = second[..., 1, :, :]
    return jnp.stack([a_re * b_re - a_im * b_im, a_re * b_im + a_im * b_re], axis=-3)

def conj(field):
    return jnp.stack([field[..., 0, :, :], -field[..., 1, :, :]], axis=-3)

def pattern_grad(window, probe, amp, valid, mats):
    k_left, k_right, f_left, f_right, kc_left, kc_right, fc_left, fc_right = mats
    psi_one = cmul(probe, window[0]).astype(jnp.bfloat16)
    upper = apply_left(k_left, psi_one).astype(jnp.bfloat16)
    phi = apply_right(upper, k_right)
    psi_two = cmul(phi, window[1]).astype(jnp.bfloat16)
    vfield = apply_left(f_left, psi_two).astype(jnp.bfloat16)
    far = apply_right(vfield, f_right)
    inten = lax.optimization_barrier(jnp.sum(far * far, axis=(0, 1)))
    ratio = amp.astype(jnp.float32) / jnp.maximum(jnp.sqrt(inten), 1.0)
    resid = (far * (valid * (1.0 - ratio))).astype(jnp.bfloat16)
    wfield = apply_left(fc_left, resid).astype(jnp.bfloat16)
    g_two = apply_right(wfield, fc_right)
    g_phi = cmul(conj(window[1]), g_two).astype(jnp.bfloat16)
    yfield = apply_left(kc_left, g_phi).astype(jnp.bfloat16)
    g_one = apply_right(yfield, kc_right)
    grad_one = lax.optimization_barrier(jnp.sum(cmul(conj(probe), g_one), axis=0))
    grad_two = lax.optimization_barrier(jnp.sum(cmul(conj(phi), g_two), axis=0))
    return jnp.stack([grad_one, grad_two])

def reference(objects, probe, amplitudes, owners, off_rows, off_cols):
    mats = make_mats(P_SIZE)
    padded = jnp.pad(objects, ((0, 0), (0, 0), (B, B), (B, B)))
    total = GRID_R * GRID_C * SRC_DEV
    row_index = jnp.arange(total, dtype=jnp.int32) // (GRID_C * SRC_DEV)
    amps = amplitudes.reshape(total, P_SIZE, P_SIZE)
    dest = owners.reshape(total).astype(jnp.int32)
    start_rows = (row_index * TH + off_rows.reshape(total)).astype(jnp.int32)
    start_cols = (dest * TW + off_cols.reshape(total)).astype(jnp.int32)

    def visit(carry, item):
        srow, scol, amp = item
        zero = jnp.zeros((), jnp.int32)
        corner = (zero, zero, srow, scol)
        window = lax.dynamic_slice(padded, corner, (SLICES, 2, P_SIZE, P_SIZE))
        grads = pattern_grad(window, probe, amp, 1.0, mats)
        current = lax.dynamic_slice(carry, corner, (SLICES, 2, P_SIZE, P_SIZE))
        return (lax.dynamic_update_slice(carry, current + grads, corner), None)
    start = jnp.zeros(padded.shape, jnp.float32)
    summed, _ = lax.scan(visit, start, (start_rows, start_cols, amps))
    return summed[:, :, B:B + OH, B:B + OW]
```

```python
import functools
import math

import jax
import jax.numpy as jnp
import numpy as np
from jax import lax
from jax.experimental import pallas as pl
from jax.experimental.pallas import tpu as pltpu
from jax.sharding import PartitionSpec as P

FRESNEL = 24.0
REACH_OFFSETS = (-3, -2, -1, 1, 2, 3, 4)
CAP = 2
LANES = 128
NOTE = 16
VMEM_BYTES = 40 * 1024 * 1024


def make_tables(width):
    idx = np.arange(width)
    angle = (idx[:, None] * idx[None, :] % width).astype(np.float32) * np.float32(2.0 * math.pi / width)
    scale = np.float32(1.0 / math.sqrt(width))
    f_re = np.cos(angle) * scale
    f_im = -np.sin(angle) * scale
    centred = (idx + width // 2) % width - width // 2
    theta = (centred * centred).astype(np.float32) * np.float32(math.pi * FRESNEL / (width * width))
    d_re = np.cos(theta)
    d_im = -np.sin(theta)
    m_re = d_re[:, None] * f_re - d_im[:, None] * f_im
    m_im = d_re[:, None] * f_im + d_im[:, None] * f_re
    k_re = f_re @ m_re + f_im @ m_im
    k_im = f_re @ m_im - f_im @ m_re
    tables = []
    for re, im in ((k_re, k_im), (f_re, f_im)):
        tables.append(np.block([[re, -im], [im, re]]))
        tables.append(np.block([[re, im], [-im, re]]))
    return jnp.asarray(np.stack(tables).astype(jnp.bfloat16))


def partners(ncols):
    if ncols == 8:
        return [[i ^ k for i in range(ncols)] for k in (4, 6, 5, 7, 2, 3, 1)]
    return [[(i + k) % ncols for i in range(ncols)] for k in REACH_OFFSETS]


def pack_kernel(kinds, count, owners, at_rows, at_cols, dests, obj, amps, *outs):
    msgs, (left, right, upper, lower) = outs[:kinds], outs[kinds:]
    rows, cols = obj.shape[1:]
    border = amps.shape[1] // 2
    lane = lax.broadcasted_iota(jnp.int32, (1, LANES), 1)
    low = lane < border
    for pair in range(2):
        even, odd = 2 * pair, 2 * pair + 1
        left[pair] = jnp.where(
            low, obj[even, :, :LANES], pltpu.roll(obj[odd, :, :LANES], border, 1)
        ).astype(jnp.bfloat16)
        right[pair] = jnp.where(
            low, pltpu.roll(obj[even, :, cols - LANES :], border, 1), obj[odd, :, cols - LANES :]
        ).astype(jnp.bfloat16)
    for plane in range(4):
        for block in range(cols // LANES):
            span = slice(block * LANES, (block + 1) * LANES)
            upper[plane, block] = obj[plane, :border, span].astype(jnp.bfloat16)
            lower[plane, block] = obj[plane, rows - border :, span].astype(jnp.bfloat16)
    width = amps.shape[1]
    row_id = lax.broadcasted_iota(jnp.int32, (NOTE, LANES), 0)
    lane_id = lax.broadcasted_iota(jnp.int32, (NOTE, LANES), 1)
    for kind in range(kinds):
        found = jnp.int32(0)
        slots = [jnp.int32(0)] * CAP
        for j in range(count):
            mine = owners[j] == dests[kind]
            for slot in range(CAP):
                slots[slot] = jnp.where(mine & (found == slot), j, slots[slot])
            found = found + mine.astype(jnp.int32)
        note = jnp.zeros((NOTE, LANES), jnp.float32)
        for slot in range(CAP):
            j = slots[slot]
            msgs[kind][slot * width : (slot + 1) * width] = amps[j]
            live = (found > slot).astype(jnp.int32)
            for place, value in enumerate((at_rows[j], at_cols[j], live)):
                here = (row_id == slot) & (lane_id == place)
                note = jnp.where(here, value.astype(jnp.float32), note)
        msgs[kind][CAP * width :] = note.astype(jnp.bfloat16)


def unpack_sides(pair, from_right, from_left, border):
    lane = lax.broadcasted_iota(jnp.int32, (1, LANES), 1)
    low = lane < border
    near = from_right[pair].astype(jnp.float32)
    far = from_left[pair].astype(jnp.float32)
    even = jnp.where(low, near, pltpu.roll(far, border, 1))
    odd = jnp.where(low, pltpu.roll(near, border, 1), far)
    return even, odd


def rows_kernel(from_right, from_left, upper, lower, up, down):
    border = upper.shape[2]
    rows = from_right.shape[1]
    blocks = upper.shape[1]
    up[:, :blocks] = upper[...]
    down[:, :blocks] = lower[...]
    for message, at in ((up, 0), (down, rows - border)):
        for pair in range(2):
            even, odd = unpack_sides(
                pair, from_right.at[:, at : at + border], from_left.at[:, at : at + border], border
            )
            message[2 * pair, blocks] = even.astype(jnp.bfloat16)
            message[2 * pair + 1, blocks] = odd.astype(jnp.bfloat16)


def matmul(first, second):
    return jnp.dot(first, second, preferred_element_type=jnp.float32)


def quarters(field):
    half = field.shape[0] // 2
    return field[:half, :half], field[:half, half:], field[half:, :half], field[half:, half:]


def joined(a, b, c, d):
    return jnp.concatenate(
        [jnp.concatenate([a, b], axis=1), jnp.concatenate([c, d], axis=1)], axis=0
    ).astype(jnp.bfloat16)


def swapped(field):
    a, b, c, d = quarters(field)
    return joined(a, c, b, d)


def main_kernel(kinds, tables, probe, obj, from_right, from_left, from_above, from_below, *refs):
    msgs = refs[:kinds]
    centre, up, down = refs[kinds : kinds + 3]
    ext, grad, amps, notes, notes_s, order, sem = refs[kinds + 3 :]
    rows, cols = obj.shape[1:]
    width = probe.shape[2]
    border = width // 2
    blocks = cols // LANES
    span = cols + 2 * border

    for kind in range(kinds):
        note = msgs[kind][CAP * width :].astype(jnp.float32).astype(jnp.int32)
        notes[kind * 8 : (kind + 1) * 8] = note[:8]
    copy = pltpu.make_async_copy(notes, notes_s, sem)
    copy.start()
    for kind in range(kinds):
        for slot in range(CAP):
            amps[kind * CAP + slot] = msgs[kind][slot * width : (slot + 1) * width]
    for plane in range(4):
        for block in range(blocks):
            ext[plane, block, border : border + rows] = obj[plane, :, block * LANES : (block + 1) * LANES]
        for block in range(blocks + 1):
            ext[plane, block, :border] = from_above[plane, block].astype(jnp.float32)
            ext[plane, block, border + rows :] = from_below[plane, block].astype(jnp.float32)
    for pair in range(2):
        even, odd = unpack_sides(pair, from_right, from_left, border)
        ext[2 * pair, blocks, border : border + rows] = even
        ext[2 * pair + 1, blocks, border : border + rows] = odd
    grad[...] = jnp.zeros_like(grad)
    copy.wait()

    total = jnp.int32(0)
    for kind in range(kinds):
        for slot in range(CAP):
            order[total] = kind * CAP + slot
            total = total + notes_s[kind * 8 + slot, 2]
    order[total] = 0

    lane = lax.broadcasted_iota(jnp.int32, (1, LANES), 1)

    def stages(items):
        places = []
        for number in items:
            which = order[number]
            kind, slot = which // CAP, which % CAP
            row = notes_s[kind * 8 + slot, 0]
            col = notes_s[kind * 8 + slot, 1]
            start = col + (span - border)
            start = jnp.where(start >= span, start - span, start)
            first = start // LANES
            shift = start % LANES
            second = jnp.where(first == blocks, 0, first + 1)
            places.append((which, row, first, second, shift))
        windows = []
        for which, row, first, second, shift in places:
            window = []
            for plane in range(4):
                a = ext[plane, first, pl.ds(row, width), :]
                b = ext[plane, second, pl.ds(row, width), :]
                both = jnp.where(lane >= shift, a, b)
                window.append(pltpu.roll(both, (LANES - shift) % LANES, 1))
            windows.append(window)
        fields = []
        for window in windows:
            parts = []
            for mode in range(2):
                p_re, p_im = probe[mode, 0], probe[mode, 1]
                parts.append((p_re * window[0] - p_im * window[1], p_re * window[1] + p_im * window[0]))
            fields.append(joined(parts[0][0], parts[1][0], parts[0][1], parts[1][1]))
        fields = [swapped(matmul(tables[0], f)) for f in fields]
        phis = [matmul(f, tables[1]) for f in fields]
        fields = []
        for window, phi in zip(windows, phis):
            a_re, a_im, b_re, b_im = quarters(phi)
            w_re, w_im = window[2], window[3]
            fields.append(
                joined(
                    a_re * w_re - a_im * w_im,
                    b_re * w_re - b_im * w_im,
                    a_re * w_im + a_im * w_re,
                    b_re * w_im + b_im * w_re,
                )
            )
        fields = [swapped(matmul(tables[2], f)) for f in fields]
        fars = [matmul(f, tables[3]) for f in fields]
        fields = []
        for place, far in zip(places, fars):
            a_re, a_im, b_re, b_im = quarters(far)
            inten = a_re * a_re + a_im * a_im + b_re * b_re + b_im * b_im
            keep = 1.0 - amps[place[0]].astype(jnp.float32) * lax.rsqrt(jnp.maximum(inten, 1.0))
            fields.append(joined(a_re * keep, b_re * keep, a_im * keep, b_im * keep))
        fields = [swapped(matmul(tables[3], f)) for f in fields]
        seconds = [matmul(f, tables[2]) for f in fields]
        fields = []
        for window, second in zip(windows, seconds):
            a_re, a_im, b_re, b_im = quarters(second)
            w_re, w_im = window[2], window[3]
            fields.append(
                joined(
                    w_re * a_re + w_im * a_im,
                    w_re * b_re + w_im * b_im,
                    w_re * a_im - w_im * a_re,
                    w_re * b_im - w_im * b_re,
                )
            )
        fields = [swapped(matmul(tables[1], f)) for f in fields]
        firsts = [matmul(f, tables[0]) for f in fields]
        for number, place, phi, one, two in zip(items, places, phis, firsts, seconds):
            _, row, first, second, shift = place
            sums = []
            probes = (probe[0, 0], probe[0, 1], probe[1, 0], probe[1, 1])
            for left, right in ((probes, one), (quarters(phi), two)):
                p_re, p_im, q_re, q_im = left
                a_re, a_im, b_re, b_im = quarters(right)
                sums.append(p_re * a_re + p_im * a_im + q_re * b_re + q_im * b_im)
                sums.append(p_re * a_im - p_im * a_re + q_re * b_im - q_im * b_re)
            live = number < total
            for plane in range(4):
                moved = pltpu.roll(sums[plane], shift, 1)
                grad[plane, first, pl.ds(row, width), :] += jnp.where((lane >= shift) & live, moved, 0.0)
                grad[plane, second, pl.ds(row, width), :] += jnp.where((lane < shift) & live, moved, 0.0)

    def visit(step, carry):
        stages((2 * step, 2 * step + 1))
        return carry

    lax.fori_loop(0, (total + 1) // 2, visit, 0)

    for plane in range(4):
        for block in range(blocks + 1):
            centre[plane, block] = grad[plane, block, border : border + rows]
            up[plane, block] = grad[plane, block, :border].astype(jnp.bfloat16)
            down[plane, block] = grad[plane, block, border + rows :].astype(jnp.bfloat16)


def sides_kernel(centre, from_above, from_below, middle, right, left):
    blocks = centre.shape[1] - 1
    rows = centre.shape[2]
    border = from_above.shape[2]
    lane = lax.broadcasted_iota(jnp.int32, (1, LANES), 1)
    low = lane < border

    def total(plane, block):
        whole = centre[plane, block]
        top = whole[:border] + from_above[plane, block].astype(jnp.float32)
        bottom = whole[rows - border :] + from_below[plane, block].astype(jnp.float32)
        return jnp.concatenate([top, whole[border : rows - border], bottom], axis=0)

    for pair in range(2):
        even, odd = total(2 * pair, blocks), total(2 * pair + 1, blocks)
        right[pair] = jnp.where(low, even, pltpu.roll(odd, border, 1)).astype(jnp.bfloat16)
        left[pair] = jnp.where(low, pltpu.roll(even, border, 1), odd).astype(jnp.bfloat16)
    for plane in range(4):
        for block in range(blocks):
            middle[plane, :, block * LANES : (block + 1) * LANES] = total(plane, block)


def final_kernel(middle, from_right, from_left, out):
    cols = middle.shape[2]
    border = LANES // 2
    lane = lax.broadcasted_iota(jnp.int32, (1, LANES), 1)
    low = lane < border
    for pair in range(2):
        near = from_left[pair].astype(jnp.float32)
        far = from_right[pair].astype(jnp.float32)
        even, odd = 2 * pair, 2 * pair + 1
        for plane, first, last in (
            (even, near, pltpu.roll(far, border, 1)),
            (odd, pltpu.roll(near, border, 1), far),
        ):
            add_first = jnp.where(low, first, 0.0)
            add_last = jnp.where(low, 0.0, last)
            if cols == LANES:
                out[plane] = middle[plane] + add_first + add_last
                continue
            out[plane, :, :LANES] = middle[plane, :, :LANES] + add_first
            if cols > 2 * LANES:
                out[plane, :, LANES : cols - LANES] = middle[plane, :, LANES : cols - LANES]
            out[plane, :, cols - LANES :] = middle[plane, :, cols - LANES :] + add_last


def local(ncols, nrows, objects, probe, amplitudes, owners, off_rows, off_cols):
    width = amplitudes.shape[-1]
    border = width // 2
    count = amplitudes.shape[2]
    rows, cols = objects.shape[2:]
    blocks = cols // LANES
    routes = partners(ncols)
    kinds = len(routes)
    myself = lax.axis_index("col")
    dests = jnp.asarray(np.array(routes, np.int32))[:, myself]
    obj = objects.reshape(4, rows, cols)
    vmem = pl.BlockSpec(memory_space=pltpu.VMEM)
    smem = pl.BlockSpec(memory_space=pltpu.SMEM)
    params = pltpu.CompilerParams(vmem_limit_bytes=VMEM_BYTES)
    bf16 = functools.partial(jax.ShapeDtypeStruct, dtype=jnp.bfloat16)
    f32 = functools.partial(jax.ShapeDtypeStruct, dtype=jnp.float32)

    def ahead(array, axis, size, step):
        return lax.ppermute(array, axis, [(i, i + step) for i in range(size) if 0 <= i + step < size])

    packed = pl.pallas_call(
        functools.partial(pack_kernel, kinds, count),
        out_shape=[bf16((CAP * width + NOTE, LANES))] * kinds
        + [bf16((2, rows, LANES))] * 2
        + [bf16((4, blocks, border, LANES))] * 2,
        in_specs=[smem] * 4 + [vmem] * 2,
        out_specs=[vmem] * (kinds + 4),
        compiler_params=params,
        name="pack",
    )(
        owners.reshape(count),
        off_rows.reshape(count),
        off_cols.reshape(count),
        dests,
        obj,
        amplitudes.reshape(count, width, width),
    )
    left, right, upper, lower = packed[kinds:]
    from_right = ahead(left, "col", ncols, -1)
    from_left = ahead(right, "col", ncols, 1)
    msgs = [
        lax.ppermute(msg, "col", list(enumerate(route)))
        for msg, route in zip(packed[:kinds], routes)
    ]
    up, down = pl.pallas_call(
        rows_kernel,
        out_shape=[bf16((4, blocks + 1, border, LANES))] * 2,
        in_specs=[vmem] * 4,
        out_specs=[vmem] * 2,
        compiler_params=params,
        name="rows",
    )(from_right, from_left, upper, lower)
    from_below = ahead(up, "row", nrows, -1)
    from_above = ahead(down, "row", nrows, 1)

    centre, up, down = pl.pallas_call(
        functools.partial(main_kernel, kinds),
        out_shape=[f32((4, blocks + 1, rows, LANES))] + [bf16((4, blocks + 1, border, LANES))] * 2,
        in_specs=[vmem] * (7 + kinds),
        out_specs=[vmem] * 3,
        scratch_shapes=[
            pltpu.VMEM((4, blocks + 1, rows + 2 * border, LANES), jnp.float32),
            pltpu.VMEM((4, blocks + 1, rows + 2 * border, LANES), jnp.float32),
            pltpu.VMEM((kinds * CAP, width, width), jnp.bfloat16),
            pltpu.VMEM((kinds * 8, LANES), jnp.int32),
            pltpu.SMEM((kinds * 8, LANES), jnp.int32),
            pltpu.SMEM((kinds * CAP + 1,), jnp.int32),
            pltpu.SemaphoreType.DMA,
        ],
        compiler_params=params,
        name="gradients",
    )(make_tables(width), probe, obj, from_right, from_left, from_above, from_below, *msgs)

    back_below = ahead(up, "row", nrows, -1)
    back_above = ahead(down, "row", nrows, 1)
    middle, right, left = pl.pallas_call(
        sides_kernel,
        out_shape=[f32((4, rows, cols))] + [bf16((2, rows, LANES))] * 2,
        in_specs=[vmem] * 3,
        out_specs=[vmem] * 3,
        compiler_params=params,
        name="sides",
    )(centre, back_above, back_below)
    back_left = ahead(right, "col", ncols, 1)
    back_right = ahead(left, "col", ncols, -1)
    out = pl.pallas_call(
        final_kernel,
        out_shape=f32((4, rows, cols)),
        in_specs=[vmem] * 3,
        out_specs=vmem,
        compiler_params=params,
        name="final",
    )(middle, back_right, back_left)
    return out.reshape(objects.shape)


def solution(mesh):
    placed = (
        P(None, None, "row", "col"),
        P(),
        P("row", "col", None, None, None),
        P("row", "col", None),
        P("row", "col", None),
        P("row", "col", None),
    )
    return jax.shard_map(
        functools.partial(local, mesh.shape["col"], mesh.shape["row"]),
        mesh=mesh,
        in_specs=placed,
        out_specs=P(None, None, "row", "col"),
        check_vma=False,
    )
```

```python
import functools
import math

import jax
import jax.numpy as jnp
import numpy as np
from jax import lax
from jax.experimental import pallas as pl
from jax.experimental.pallas import tpu as pltpu
from jax.sharding import PartitionSpec as P

FRESNEL = 24.0
REACH_OFFSETS = (-3, -2, -1, 1, 2, 3, 4)
CAP = 2
LANES = 128
NOTE = 16
VMEM_BYTES = 40 * 1024 * 1024
FULL_BYTES = 60 * 1024 * 1024


def make_tables(width):
    idx = np.arange(width)
    angle = (idx[:, None] * idx[None, :] % width).astype(np.float32) * np.float32(2.0 * math.pi / width)
    scale = np.float32(1.0 / math.sqrt(width))
    f_re = np.cos(angle) * scale
    f_im = -np.sin(angle) * scale
    centred = (idx + width // 2) % width - width // 2
    theta = (centred * centred).astype(np.float32) * np.float32(math.pi * FRESNEL / (width * width))
    d_re = np.cos(theta)
    d_im = -np.sin(theta)
    m_re = d_re[:, None] * f_re - d_im[:, None] * f_im
    m_im = d_re[:, None] * f_im + d_im[:, None] * f_re
    k_re = f_re @ m_re + f_im @ m_im
    k_im = f_re @ m_im - f_im @ m_re
    tables = []
    for re, im in ((k_re, k_im), (f_re, f_im)):
        tables.append(np.block([[re, -im], [im, re]]))
        tables.append(np.block([[re, im], [-im, re]]))
    return jnp.asarray(np.stack(tables).astype(jnp.bfloat16))


def row_partners(nrows, ncols):
    first = [((r, c), (r ^ 1, c)) for r in range(nrows) for c in range(ncols)]
    second = []
    for r in range(nrows):
        other = ((r + 1) ^ 1) - 1
        for c in range(ncols):
            second.append(((r, c), (other, c) if 0 <= other < nrows else (r, c ^ 1)))
    return first, second


def meet(at, step, turn, size):
    odd = (at // 2 if step == 2 else at) % 2
    return (at + size + step * (1 - 2 * odd) * (1 - 2 * turn)) % size


def routes(ncols):
    paired = [
        functools.partial(lambda step, turn, at: meet(at, step, turn, ncols), step, turn)
        for step in (1, 2, 3)
        for turn in (0, 1)
    ]
    return paired + [lambda at: (at + 4) % ncols]


def col_partners(nrows, ncols):
    first = [((r, c), (r, c ^ 1)) for r in range(nrows) for c in range(ncols)]
    second = []
    for c in range(ncols):
        other = ((c + 1) ^ 1) - 1
        for r in range(nrows):
            second.append(((r, c), (r, other) if 0 <= other < ncols else (r ^ 1, c)))
    return first, second


def sides(axis, size):
    at = lax.axis_index(axis)
    return at % 2 == 0, (at > 0) & (at < size - 1)


def join_right(even, odd, border):
    low = lax.broadcasted_iota(jnp.int32, (1, LANES), 1) < border
    return jnp.where(low, even, pltpu.roll(odd, border, 1))


def join_left(even, odd, border):
    low = lax.broadcasted_iota(jnp.int32, (1, LANES), 1) < border
    return jnp.where(low, pltpu.roll(even, border, 1), odd)


def pack_kernel(ways, ncols, amps, owners, at_rows, at_cols, obj, *refs):
    side_one, side_two, msgs, tile, held, ints, sem = refs
    count, width = held.shape[:2]
    rows, cols = obj.shape[2:]
    border = width // 2
    copies = [
        pltpu.make_async_copy(ref, ints.at[number], sem.at[number])
        for number, ref in enumerate((owners, at_rows, at_cols))
    ]
    copies.append(pltpu.make_async_copy(obj, tile, sem.at[3]))
    copies.append(pltpu.make_async_copy(amps.at[0, 0], held, sem.at[4]))
    for copy in copies:
        copy.start()
    for copy in copies:
        copy.wait()

    myself = lax.axis_index("col")
    even_col, _ = sides("col", ncols)
    for pair in range(2):
        planes = (tile.at[pair, 0], tile.at[pair, 1])
        left = join_right(*(plane[:, :LANES] for plane in planes), border)
        right = join_left(*(plane[:, cols - LANES :] for plane in planes), border)
        side_one[pair] = jnp.where(even_col, right, left).astype(jnp.bfloat16)
        side_two[pair] = jnp.where(even_col, left, right).astype(jnp.bfloat16)
    row_id = lax.broadcasted_iota(jnp.int32, (NOTE, LANES), 0)
    lane_id = lax.broadcasted_iota(jnp.int32, (NOTE, LANES), 1)
    for kind, way in enumerate(ways):
        owner = way(myself)
        found = jnp.int32(0)
        slots = [jnp.int32(0)] * CAP
        for j in range(count):
            mine = ints[0, 0, 0, j] == owner
            for slot in range(CAP):
                slots[slot] = jnp.where(mine & (found == slot), j, slots[slot])
            found = found + mine.astype(jnp.int32)
        note = jnp.zeros((NOTE, LANES), jnp.float32)
        for slot in range(CAP):
            j = slots[slot]
            msgs[kind, slot * width : (slot + 1) * width] = held[j]
            live = (found > slot).astype(jnp.int32)
            for lane, value in enumerate((ints[1, 0, 0, j], ints[2, 0, 0, j], live)):
                here = (row_id == slot) & (lane_id == lane)
                note = jnp.where(here, value.astype(jnp.float32), note)
        msgs[kind, CAP * width :] = note.astype(jnp.bfloat16)


def rows_kernel(ncols, nrows, came_one, came_two, obj, side, row_one, row_two):
    rows = side.shape[1]
    border = row_two.shape[2]
    blocks = row_two.shape[1] - 1
    even_col, inner = sides("col", ncols)
    even_row, _ = sides("row", nrows)
    for pair in range(2):
        one = came_one[pair].astype(jnp.float32)
        two = jnp.where(inner, came_two[pair].astype(jnp.float32), 0.0)
        near = jnp.where(even_col, one, two)
        far = jnp.where(even_col, two, one)
        side[2 * pair] = join_right(near, far, border).astype(jnp.bfloat16)
        side[2 * pair + 1] = join_left(near, far, border).astype(jnp.bfloat16)
    low = pl.multiple_of(jnp.where(even_row, rows - border, 0), border)
    high = pl.multiple_of(jnp.where(even_row, 0, rows - border), border)
    for message, start in ((row_one, low), (row_two, high)):
        for plane in range(4):
            for block in range(blocks):
                here = obj[plane, pl.ds(start, border), block * LANES : (block + 1) * LANES]
                message[plane, block] = here.astype(jnp.bfloat16)
            message[plane, blocks] = side[plane, pl.ds(start, border), :]


def matmul(first, second):
    return jnp.dot(first, second, preferred_element_type=jnp.float32)


def quarters(field):
    half = field.shape[0] // 2
    return field[:half, :half], field[:half, half:], field[half:, :half], field[half:, half:]


def joined(a, b, c, d):
    return jnp.concatenate(
        [jnp.concatenate([a, b], axis=1), jnp.concatenate([c, d], axis=1)], axis=0
    ).astype(jnp.bfloat16)


def swapped(field):
    a, b, c, d = quarters(field)
    return joined(a, c, b, d)


def main_kernel(ncols, nrows, tables, probe, obj, side, row_one, row_two, msgs, *refs):
    centre, out_one, out_two, mid_one, mid_two, ext, grad, notes, notes_s, order, sem = refs
    kinds = msgs.shape[0]
    rows, cols = obj.shape[1:]
    width = probe.shape[2]
    border = width // 2
    blocks = cols // LANES
    span = cols + 2 * border
    even_row, inner = sides("row", nrows)
    after_one = pl.multiple_of(jnp.where(even_row, border + rows, 0), border)
    after_two = pl.multiple_of(jnp.where(even_row, 0, border + rows), border)

    for kind in range(kinds):
        note = msgs[kind, CAP * width :].astype(jnp.float32).astype(jnp.int32)
        notes[kind * 8 : (kind + 1) * 8] = note[:8]
    copy = pltpu.make_async_copy(notes, notes_s, sem)
    copy.start()
    for plane in range(4):
        for block in range(blocks):
            ext[plane, block, border : border + rows] = obj[plane, :, block * LANES : (block + 1) * LANES]
        ext[plane, blocks, border : border + rows] = side[plane].astype(jnp.float32)
        for block in range(blocks + 1):
            ext[plane, block, pl.ds(after_one, border), :] = row_one[plane, block].astype(jnp.float32)
            ext[plane, block, pl.ds(after_two, border), :] = jnp.where(
                inner, row_two[plane, block].astype(jnp.float32), 0.0
            )
    grad[...] = jnp.zeros_like(grad)
    copy.wait()

    total = jnp.int32(0)
    for kind in range(kinds):
        for slot in range(CAP):
            order[total] = kind * CAP + slot
            total = total + notes_s[kind * 8 + slot, 2]
    order[total] = 0

    lane = lax.broadcasted_iota(jnp.int32, (1, LANES), 1)

    def stages(items):
        places = []
        for number in items:
            which = order[number]
            kind, slot = which // CAP, which % CAP
            row = notes_s[kind * 8 + slot, 0]
            col = notes_s[kind * 8 + slot, 1]
            start = col + (span - border)
            start = jnp.where(start >= span, start - span, start)
            first = start // LANES
            shift = start % LANES
            second = jnp.where(first == blocks, 0, first + 1)
            places.append((kind, slot, row, first, second, shift))
        windows = []
        for _, _, row, first, second, shift in places:
            window = []
            for plane in range(4):
                a = ext[plane, first, pl.ds(row, width), :]
                b = ext[plane, second, pl.ds(row, width), :]
                both = jnp.where(lane >= shift, a, b)
                window.append(pltpu.roll(both, (LANES - shift) % LANES, 1))
            windows.append(window)
        fields = []
        for window in windows:
            parts = []
            for mode in range(2):
                p_re, p_im = probe[mode, 0], probe[mode, 1]
                parts.append((p_re * window[0] - p_im * window[1], p_re * window[1] + p_im * window[0]))
            fields.append(joined(parts[0][0], parts[1][0], parts[0][1], parts[1][1]))
        fields = [swapped(matmul(tables[0], f)) for f in fields]
        phis = [matmul(f, tables[1]) for f in fields]
        fields = []
        for window, phi in zip(windows, phis):
            a_re, a_im, b_re, b_im = quarters(phi)
            w_re, w_im = window[2], window[3]
            fields.append(
                joined(
                    a_re * w_re - a_im * w_im,
                    b_re * w_re - b_im * w_im,
                    a_re * w_im + a_im * w_re,
                    b_re * w_im + b_im * w_re,
                )
            )
        fields = [swapped(matmul(tables[2], f)) for f in fields]
        fars = [matmul(f, tables[3]) for f in fields]
        fields = []
        for place, far in zip(places, fars):
            a_re, a_im, b_re, b_im = quarters(far)
            inten = a_re * a_re + a_im * a_im + b_re * b_re + b_im * b_im
            kind, slot = place[:2]
            amp = msgs[kind, pl.ds(pl.multiple_of(slot * width, width), width), :].astype(jnp.float32)
            keep = 1.0 - amp * lax.rsqrt(jnp.maximum(inten, 1.0))
            fields.append(joined(a_re * keep, b_re * keep, a_im * keep, b_im * keep))
        fields = [swapped(matmul(tables[3], f)) for f in fields]
        seconds = [matmul(f, tables[2]) for f in fields]
        fields = []
        for window, second in zip(windows, seconds):
            a_re, a_im, b_re, b_im = quarters(second)
            w_re, w_im = window[2], window[3]
            fields.append(
                joined(
                    w_re * a_re + w_im * a_im,
                    w_re * b_re + w_im * b_im,
                    w_re * a_im - w_im * a_re,
                    w_re * b_im - w_im * b_re,
                )
            )
        fields = [swapped(matmul(tables[1], f)) for f in fields]
        firsts = [matmul(f, tables[0]) for f in fields]
        for number, place, phi, one, two in zip(items, places, phis, firsts, seconds):
            _, _, row, first, second, shift = place
            sums = []
            probes = (probe[0, 0], probe[0, 1], probe[1, 0], probe[1, 1])
            for left, right in ((probes, one), (quarters(phi), two)):
                p_re, p_im, q_re, q_im = left
                a_re, a_im, b_re, b_im = quarters(right)
                sums.append(p_re * a_re + p_im * a_im + q_re * b_re + q_im * b_im)
                sums.append(p_re * a_im - p_im * a_re + q_re * b_im - q_im * b_re)
            live = number < total
            for plane in range(4):
                moved = pltpu.roll(sums[plane], shift, 1)
                grad[plane, first, pl.ds(row, width), :] += jnp.where((lane >= shift) & live, moved, 0.0)
                grad[plane, second, pl.ds(row, width), :] += jnp.where((lane < shift) & live, moved, 0.0)

    def visit(step, carry):
        stages((2 * step, 2 * step + 1))
        return carry

    lax.fori_loop(0, (total + 1) // 2, visit, 0)

    for plane in range(4):
        for block in range(blocks + 1):
            centre[plane, block] = grad[plane, block, border : border + rows]
            out_one[plane, block] = grad[plane, block, pl.ds(after_one, border), :].astype(jnp.bfloat16)
            out_two[plane, block] = grad[plane, block, pl.ds(after_two, border), :].astype(jnp.bfloat16)
    even_col, _ = sides("col", ncols)
    middle = slice(2 * border, rows)
    for pair in range(2):
        even, odd = grad[2 * pair, blocks, middle], grad[2 * pair + 1, blocks, middle]
        right, left = join_right(even, odd, border), join_left(even, odd, border)
        mid_one[pair] = jnp.where(even_col, right, left).astype(jnp.bfloat16)
        mid_two[pair] = jnp.where(even_col, left, right).astype(jnp.bfloat16)


def sides_kernel(ncols, nrows, centre, came_one, came_two, middle, side_one, side_two):
    blocks = centre.shape[1] - 1
    rows = centre.shape[2]
    border = came_one.shape[2]
    even_col, _ = sides("col", ncols)
    even_row, inner = sides("row", nrows)

    def ends(plane, block):
        one = came_one[plane, block].astype(jnp.float32)
        two = jnp.where(inner, came_two[plane, block].astype(jnp.float32), 0.0)
        top = centre[plane, block, :border] + jnp.where(even_row, two, one)
        bottom = centre[plane, block, rows - border :] + jnp.where(even_row, one, two)
        return top, bottom

    for pair in range(2):
        for number, (even, odd) in enumerate(zip(ends(2 * pair, blocks), ends(2 * pair + 1, blocks))):
            right, left = join_right(even, odd, border), join_left(even, odd, border)
            span = slice(number * border, (number + 1) * border)
            side_one[pair, span] = jnp.where(even_col, right, left).astype(jnp.bfloat16)
            side_two[pair, span] = jnp.where(even_col, left, right).astype(jnp.bfloat16)
    for plane in range(4):
        for block in range(blocks):
            span = slice(block * LANES, (block + 1) * LANES)
            top, bottom = ends(plane, block)
            middle[plane, :border, span] = top
            middle[plane, border : rows - border, span] = centre[plane, block, border : rows - border]
            middle[plane, rows - border :, span] = bottom


def final_kernel(ncols, border, middle, mid_one, mid_two, end_one, end_two, out):
    rows, cols = middle.shape[1:]
    low = lax.broadcasted_iota(jnp.int32, (1, LANES), 1) < border
    even_col, inner = sides("col", ncols)
    parts = (
        (slice(0, border), end_one, end_two, slice(0, border)),
        (slice(border, rows - border), mid_one, mid_two, slice(0, rows - 2 * border)),
        (slice(rows - border, rows), end_one, end_two, slice(border, 2 * border)),
    )
    for span, came_one, came_two, source in parts:
        for pair in range(2):
            one = came_one[pair, source].astype(jnp.float32)
            two = jnp.where(inner, came_two[pair, source].astype(jnp.float32), 0.0)
            near = jnp.where(even_col, two, one)
            far = jnp.where(even_col, one, two)
            even, odd = 2 * pair, 2 * pair + 1
            for plane, first, last in (
                (even, near, pltpu.roll(far, border, 1)),
                (odd, pltpu.roll(near, border, 1), far),
            ):
                add_first = jnp.where(low, first, 0.0)
                add_last = jnp.where(low, 0.0, last)
                if cols == LANES:
                    out[plane, span] = middle[plane, span] + add_first + add_last
                    continue
                out[plane, span, :LANES] = middle[plane, span, :LANES] + add_first
                if cols > 2 * LANES:
                    out[plane, span, LANES : cols - LANES] = middle[plane, span, LANES : cols - LANES]
                out[plane, span, cols - LANES :] = middle[plane, span, cols - LANES :] + add_last


def local(ncols, nrows, objects, probe, amplitudes, owners, off_rows, off_cols):
    width = amplitudes.shape[-1]
    border = width // 2
    count = amplitudes.shape[2]
    rows, cols = objects.shape[2:]
    blocks = cols // LANES
    obj = objects.reshape(4, rows, cols)
    vmem = pl.BlockSpec(memory_space=pltpu.VMEM)
    anywhere = pl.BlockSpec(memory_space=pl.ANY)
    bf16 = functools.partial(jax.ShapeDtypeStruct, dtype=jnp.bfloat16)
    f32 = functools.partial(jax.ShapeDtypeStruct, dtype=jnp.float32)

    def kernel(body, ins, outs, name, scratch=(), spec=vmem, limit=VMEM_BYTES, cost=None):
        return pl.pallas_call(
            body,
            out_shape=outs,
            in_specs=[spec] * ins,
            out_specs=[vmem] * len(outs),
            scratch_shapes=list(scratch),
            compiler_params=pltpu.CompilerParams(vmem_limit_bytes=limit),
            cost_estimate=cost,
            name=name,
        )

    def across(array, way):
        return lax.ppermute(array, "col", [(i, way(i)) for i in range(ncols)])

    def swap(array, pairs):
        flat = [(a * ncols + b, c * ncols + d) for (a, b), (c, d) in pairs]
        return lax.ppermute(array, ("row", "col"), flat)

    row_one, row_two = row_partners(nrows, ncols)
    col_one, col_two = col_partners(nrows, ncols)
    if ncols == 8:
        ways = [functools.partial(lambda to, at: to, to) for to in range(ncols)]
    else:
        ways = routes(ncols)
    kinds = len(ways)
    line_shape = bf16((4, blocks + 1, border, LANES))
    side_shape = bf16((2, rows, LANES))

    side_one, side_two, msgs = kernel(
        functools.partial(pack_kernel, ways, ncols),
        5,
        [side_shape] * 2 + [bf16((kinds, CAP * width + NOTE, LANES))],
        "pack",
        [
            pltpu.VMEM(objects.shape, jnp.float32),
            pltpu.VMEM((count, width, width), jnp.bfloat16),
            pltpu.SMEM((3,) + owners.shape, jnp.int32),
            pltpu.SemaphoreType.DMA((5,)),
        ],
        anywhere,
        FULL_BYTES,
    )(amplitudes, owners, off_rows, off_cols, objects)
    came_one, came_two = swap(side_one, col_one), swap(side_two, col_two)
    if ncols == 8:
        msgs = lax.all_to_all(msgs, "col", 0, 0)
    else:
        msgs = jnp.stack([across(msgs[kind], way) for kind, way in enumerate(ways)])
    side, line_one, line_two = kernel(
        functools.partial(rows_kernel, ncols, nrows),
        3,
        [bf16((4, rows, LANES))] + [line_shape] * 2,
        "rows",
        cost=pl.CostEstimate(flops=10**12, bytes_accessed=10**9, transcendentals=10**9),
    )(came_one, came_two, obj)
    line_one, line_two = swap(line_one, row_one), swap(line_two, row_two)

    whole = pltpu.VMEM((4, blocks + 1, rows + 2 * border, LANES), jnp.float32)
    centre, line_one, line_two, mid_one, mid_two = kernel(
        functools.partial(main_kernel, ncols, nrows),
        7,
        [f32((4, blocks + 1, rows, LANES))] + [line_shape] * 2 + [bf16((2, rows - 2 * border, LANES))] * 2,
        "gradients",
        [
            whole,
            whole,
            pltpu.VMEM((kinds * 8, LANES), jnp.int32),
            pltpu.SMEM((kinds * 8, LANES), jnp.int32),
            pltpu.SMEM((kinds * CAP + 1,), jnp.int32),
            pltpu.SemaphoreType.DMA,
        ],
    )(make_tables(width), probe, obj, side, line_one, line_two, msgs)

    line_two, line_one = swap(line_two, row_two), swap(line_one, row_one)
    mid_one, mid_two = swap(mid_one, col_one), swap(mid_two, col_two)
    middle, end_one, end_two = kernel(
        functools.partial(sides_kernel, ncols, nrows),
        3,
        [f32((4, rows, cols))] + [bf16((2, 2 * border, LANES))] * 2,
        "sides",
    )(centre, line_one, line_two)
    end_one, end_two = swap(end_one, col_one), swap(end_two, col_two)
    (out,) = kernel(
        functools.partial(final_kernel, ncols, border), 5, [f32((4, rows, cols))], "final"
    )(middle, mid_one, mid_two, end_one, end_two)
    return out.reshape(objects.shape)


def solution(mesh):
    placed = (
        P(None, None, "row", "col"),
        P(),
        P("row", "col", None, None, None),
        P("row", "col", None),
        P("row", "col", None),
        P("row", "col", None),
    )
    return jax.shard_map(
        functools.partial(local, mesh.shape["col"], mesh.shape["row"]),
        mesh=mesh,
        in_specs=placed,
        out_specs=P(None, None, "row", "col"),
        check_vma=False,
    )
```

```python
import functools
import math

import jax
import jax.numpy as jnp
import numpy as np
from jax import lax
from jax.experimental import pallas as pl
from jax.experimental.pallas import tpu as pltpu
from jax.sharding import PartitionSpec as P

FRESNEL = 24.0
REACH_OFFSETS = (-3, -2, -1, 1, 2, 3, 4)
CAP = 2
LANES = 128
NOTE = 16
FIELDS = 4
VMEM_BYTES = 40 * 1024 * 1024
FULL_BYTES = 60 * 1024 * 1024
MAIN_BYTES = 48 * 1024 * 1024
BATCH = 6
HEAVY = pl.CostEstimate(flops=10**12, bytes_accessed=10**9, transcendentals=10**9)


def make_tables(width):
    idx = np.arange(width)
    angle = (idx[:, None] * idx[None, :] % width).astype(np.float32) * np.float32(2.0 * math.pi / width)
    scale = np.float32(1.0 / math.sqrt(width))
    f_re = np.cos(angle) * scale
    f_im = -np.sin(angle) * scale
    centred = (idx + width // 2) % width - width // 2
    theta = (centred * centred).astype(np.float32) * np.float32(math.pi * FRESNEL / (width * width))
    d_re = np.cos(theta)
    d_im = -np.sin(theta)
    m_re = d_re[:, None] * f_re - d_im[:, None] * f_im
    m_im = d_re[:, None] * f_im + d_im[:, None] * f_re
    k_re = f_re @ m_re + f_im @ m_im
    k_im = f_re @ m_im - f_im @ m_re
    tables = []
    for re, im in ((k_re, k_im), (f_re, f_im)):
        tables.append(np.block([[re, -im], [im, re]]))
        tables.append(np.block([[re, im], [-im, re]]))
    return jnp.asarray(np.stack(tables).astype(jnp.bfloat16))


def row_partners(nrows, ncols, idle):
    first = [((r, c), (r ^ 1, c)) for r in range(nrows) for c in range(ncols)]
    second = []
    for r in range(nrows):
        other = ((r + 1) ^ 1) - 1
        for c in range(ncols):
            second.append(((r, c), (other, c) if 0 <= other < nrows else idle(r, c)))
    return first, second


def col_partners(nrows, ncols):
    first = [((r, c), (r, c ^ 1)) for r in range(nrows) for c in range(ncols)]
    second = []
    for c in range(ncols):
        other = ((c + 1) ^ 1) - 1
        for r in range(nrows):
            second.append(((r, c), (r, other) if 0 <= other < ncols else (r ^ 1, c)))
    return first, second


def meet(at, step, turn, size):
    odd = (at // 2 if step == 2 else at) % 2
    return (at + size + step * (1 - 2 * odd) * (1 - 2 * turn)) % size


def routes(ncols):
    paired = [
        functools.partial(lambda step, turn, at: meet(at, step, turn, ncols), step, turn)
        for step in (1, 2, 3)
        for turn in (0, 1)
    ]
    return paired + [lambda at: (at + 4) % ncols]


def sides(axis, size):
    at = lax.axis_index(axis)
    return at % 2 == 0, (at > 0) & (at < size - 1)


def join_right(even, odd, border):
    low = lax.broadcasted_iota(jnp.int32, (1, LANES), 1) < border
    return jnp.where(low, even, pltpu.roll(odd, border, 1))


def join_left(even, odd, border):
    low = lax.broadcasted_iota(jnp.int32, (1, LANES), 1) < border
    return jnp.where(low, pltpu.roll(even, border, 1), odd)


def pack_kernel(ways, ncols, amps, owners, at_rows, at_cols, obj, *refs):
    side_one, side_two, msgs, tile, held, ints, sem = refs
    count, width = held.shape[:2]
    rows, cols = obj.shape[2:]
    border = width // 2
    copies = [
        pltpu.make_async_copy(ref, ints.at[number], sem.at[number])
        for number, ref in enumerate((owners, at_rows, at_cols))
    ]
    copies.append(pltpu.make_async_copy(obj, tile, sem.at[3]))
    copies.append(pltpu.make_async_copy(amps.at[0, 0], held, sem.at[4]))
    for copy in copies:
        copy.start()
    for copy in copies:
        copy.wait()

    myself = lax.axis_index("col")
    even_col, _ = sides("col", ncols)
    for pair in range(2):
        planes = (tile.at[pair, 0], tile.at[pair, 1])
        left = join_right(*(plane[:, :LANES] for plane in planes), border)
        right = join_left(*(plane[:, cols - LANES :] for plane in planes), border)
        side_one[pair] = jnp.where(even_col, right, left).astype(jnp.bfloat16)
        side_two[pair] = jnp.where(even_col, left, right).astype(jnp.bfloat16)
    lane_id = lax.broadcasted_iota(jnp.int32, (NOTE, LANES), 1)
    for kind, way in enumerate(ways):
        owner = way(myself)
        found = jnp.int32(0)
        slots = [jnp.int32(0)] * CAP
        for j in range(count):
            mine = ints[0, 0, 0, j] == owner
            for slot in range(CAP):
                slots[slot] = jnp.where(mine & (found == slot), j, slots[slot])
            found = found + mine.astype(jnp.int32)
        note = jnp.zeros((NOTE, LANES), jnp.float32)
        for slot in range(CAP):
            j = slots[slot]
            msgs[kind, slot * width : (slot + 1) * width] = held[j]
            live = (found > slot).astype(jnp.int32)
            for field, value in enumerate((ints[1, 0, 0, j], ints[2, 0, 0, j], live)):
                here = lane_id == slot * FIELDS + field
                note = jnp.where(here, value.astype(jnp.float32), note)
        msgs[kind, CAP * width :] = note.astype(jnp.bfloat16)


def rows_kernel(ncols, nrows, came_one, came_two, obj, side, row_one, row_two):
    rows = side.shape[1]
    border = row_two.shape[2]
    blocks = row_two.shape[1] - 1
    even_col, inner = sides("col", ncols)
    even_row, _ = sides("row", nrows)
    for pair in range(2):
        one = came_one[pair].astype(jnp.float32)
        two = jnp.where(inner, came_two[pair].astype(jnp.float32), 0.0)
        near = jnp.where(even_col, one, two)
        far = jnp.where(even_col, two, one)
        side[2 * pair] = join_right(near, far, border).astype(jnp.bfloat16)
        side[2 * pair + 1] = join_left(near, far, border).astype(jnp.bfloat16)
    low = pl.multiple_of(jnp.where(even_row, rows - border, 0), border)
    high = pl.multiple_of(jnp.where(even_row, 0, rows - border), border)
    for message, start in ((row_one, low), (row_two, high)):
        for plane in range(4):
            for block in range(blocks):
                here = obj[plane, pl.ds(start, border), block * LANES : (block + 1) * LANES]
                message[plane, block] = here.astype(jnp.bfloat16)
            message[plane, blocks] = side[plane, pl.ds(start, border), :]


def matmul(first, second):
    return jnp.dot(first, second, preferred_element_type=jnp.float32)


def quarters(field):
    half = field.shape[0] // 2
    return field[:half, :half], field[:half, half:], field[half:, :half], field[half:, half:]


def joined(a, b, c, d):
    return jnp.concatenate(
        [jnp.concatenate([a, b], axis=1), jnp.concatenate([c, d], axis=1)], axis=0
    ).astype(jnp.bfloat16)


def swapped(field):
    a, b, c, d = quarters(field)
    return joined(a, c, b, d)


def after_rows(nrows, rows, border):
    even_row, inner = sides("row", nrows)
    one = pl.multiple_of(jnp.where(even_row, border + rows, 0), border)
    two = pl.multiple_of(jnp.where(even_row, 0, border + rows), border)
    return one, two, inner


def extend_kernel(nrows, obj, side, row_one, row_two, ext):
    rows, cols = obj.shape[1:]
    border = row_one.shape[2]
    blocks = cols // LANES
    after_one, after_two, inner = after_rows(nrows, rows, border)
    for plane in range(4):
        for block in range(blocks):
            ext[plane, block, border : border + rows] = obj[plane, :, block * LANES : (block + 1) * LANES]
        ext[plane, blocks, border : border + rows] = side[plane].astype(jnp.float32)
        for block in range(blocks + 1):
            ext[plane, block, pl.ds(after_one, border), :] = row_one[plane, block].astype(jnp.float32)
            ext[plane, block, pl.ds(after_two, border), :] = jnp.where(
                inner, row_two[plane, block].astype(jnp.float32), 0.0
            )


def main_kernel(batch, ncols, nrows, *refs):
    (given_tables, given_probe, given_msgs, given_ext), refs = refs[:4], refs[4:]
    (grad, out_one, out_two, mid_one, mid_two), refs = refs[:5], refs[5:]
    tables, probe, msgs, ext, notes, notes_s, order, sem = refs
    kinds = msgs.shape[0]
    width = probe.shape[2]
    border = width // 2
    blocks = ext.shape[1] - 1
    rows = ext.shape[2] - 2 * border
    span = (blocks + 1) * LANES

    copies = [
        pltpu.make_async_copy(
            given_msgs.at[:, pl.ds(CAP * width, NOTE)], msgs.at[:, pl.ds(CAP * width, NOTE)], sem.at[0]
        ),
        pltpu.make_async_copy(given_ext, ext, sem.at[5]),
        pltpu.make_async_copy(given_tables, tables, sem.at[1]),
        pltpu.make_async_copy(given_probe, probe, sem.at[2]),
        pltpu.make_async_copy(
            given_msgs.at[:, pl.ds(0, CAP * width)], msgs.at[:, pl.ds(0, CAP * width)], sem.at[3]
        ),
    ]
    for copy in copies:
        copy.start()
    grad[...] = jnp.zeros_like(grad)
    copies[0].wait()
    for kind in range(kinds):
        note = msgs[kind, CAP * width :].astype(jnp.float32).astype(jnp.int32)
        notes[kind : kind + 1] = note[:1]
    copy = pltpu.make_async_copy(notes, notes_s, sem.at[4])
    copy.start()
    copy.wait()
    total = jnp.int32(0)
    for kind in range(kinds):
        for slot in range(CAP):
            order[total] = kind * CAP + slot
            total = total + notes_s[kind, slot * FIELDS + 2]
    for spare in range(batch):
        order[total + spare] = 0

    lane = lax.broadcasted_iota(jnp.int32, (1, LANES), 1)

    def stages(items):
        places = []
        for number in items:
            kind, slot = order[number] // CAP, order[number] % CAP
            row = notes_s[kind, slot * FIELDS]
            col = notes_s[kind, slot * FIELDS + 1]
            start = col + (span - border)
            start = jnp.where(start >= span, start - span, start)
            first = start // LANES
            shift = start % LANES
            second = jnp.where(first == blocks, 0, first + 1)
            places.append((kind, slot, row, first, second, shift))
        windows = []
        for _, _, row, first, second, shift in places:
            window = []
            for plane in range(4):
                a = ext[plane, first, pl.ds(row, width), :]
                b = ext[plane, second, pl.ds(row, width), :]
                both = jnp.where(lane >= shift, a, b)
                window.append(pltpu.roll(both, (LANES - shift) % LANES, 1))
            windows.append(window)
        fields = []
        for window in windows:
            parts = []
            for mode in range(2):
                p_re, p_im = probe[mode, 0], probe[mode, 1]
                parts.append((p_re * window[0] - p_im * window[1], p_re * window[1] + p_im * window[0]))
            fields.append(joined(parts[0][0], parts[1][0], parts[0][1], parts[1][1]))
        fields = [swapped(matmul(tables[0], f)) for f in fields]
        phis = [matmul(f, tables[1]) for f in fields]
        fields = []
        for window, phi in zip(windows, phis):
            a_re, a_im, b_re, b_im = quarters(phi)
            w_re, w_im = window[2], window[3]
            fields.append(
                joined(
                    a_re * w_re - a_im * w_im,
                    b_re * w_re - b_im * w_im,
                    a_re * w_im + a_im * w_re,
                    b_re * w_im + b_im * w_re,
                )
            )
        fields = [swapped(matmul(tables[2], f)) for f in fields]
        fars = [matmul(f, tables[3]) for f in fields]
        fields = []
        for place, far in zip(places, fars):
            a_re, a_im, b_re, b_im = quarters(far)
            inten = a_re * a_re + a_im * a_im + b_re * b_re + b_im * b_im
            kind, slot = place[:2]
            amp = msgs[kind, pl.ds(pl.multiple_of(slot * width, width), width), :].astype(jnp.float32)
            keep = 1.0 - amp * lax.rsqrt(jnp.maximum(inten, 1.0))
            fields.append(joined(a_re * keep, b_re * keep, a_im * keep, b_im * keep))
        fields = [swapped(matmul(tables[3], f)) for f in fields]
        seconds = [matmul(f, tables[2]) for f in fields]
        fields = []
        for window, second in zip(windows, seconds):
            a_re, a_im, b_re, b_im = quarters(second)
            w_re, w_im = window[2], window[3]
            fields.append(
                joined(
                    w_re * a_re + w_im * a_im,
                    w_re * b_re + w_im * b_im,
                    w_re * a_im - w_im * a_re,
                    w_re * b_im - w_im * b_re,
                )
            )
        fields = [swapped(matmul(tables[1], f)) for f in fields]
        firsts = [matmul(f, tables[0]) for f in fields]
        for number, place, phi, one, two in zip(items, places, phis, firsts, seconds):
            _, _, row, first, second, shift = place
            sums = []
            probes = (probe[0, 0], probe[0, 1], probe[1, 0], probe[1, 1])
            for left, right in ((probes, one), (quarters(phi), two)):
                p_re, p_im, q_re, q_im = left
                a_re, a_im, b_re, b_im = quarters(right)
                sums.append(p_re * a_re + p_im * a_im + q_re * b_re + q_im * b_im)
                sums.append(p_re * a_im - p_im * a_re + q_re * b_im - q_im * b_re)
            live = number < total
            for plane in range(4):
                moved = pltpu.roll(sums[plane], shift, 1)
                grad[plane, first, pl.ds(row, width), :] += jnp.where((lane >= shift) & live, moved, 0.0)
                grad[plane, second, pl.ds(row, width), :] += jnp.where((lane < shift) & live, moved, 0.0)

    def visit(step, carry):
        stages([batch * step + item for item in range(batch)])
        return carry

    for copy in copies[1:]:
        copy.wait()
    lax.fori_loop(0, (total + batch - 1) // batch, visit, 0)

    after_one, after_two, _ = after_rows(nrows, rows, border)
    for plane in range(4):
        for block in range(blocks + 1):
            out_one[plane, block] = grad[plane, block, pl.ds(after_one, border), :].astype(jnp.bfloat16)
            out_two[plane, block] = grad[plane, block, pl.ds(after_two, border), :].astype(jnp.bfloat16)
    even_col, _ = sides("col", ncols)
    middle = slice(2 * border, rows)
    for pair in range(2):
        even, odd = grad[2 * pair, blocks, middle], grad[2 * pair + 1, blocks, middle]
        right, left = join_right(even, odd, border), join_left(even, odd, border)
        mid_one[pair] = jnp.where(even_col, right, left).astype(jnp.bfloat16)
        mid_two[pair] = jnp.where(even_col, left, right).astype(jnp.bfloat16)


def sides_kernel(ncols, nrows, grad, came_one, came_two, middle, side_one, side_two):
    blocks = grad.shape[1] - 1
    border = came_one.shape[2]
    rows = grad.shape[2] - 2 * border
    even_col, _ = sides("col", ncols)
    even_row, inner = sides("row", nrows)

    def ends(plane, block):
        one = came_one[plane, block].astype(jnp.float32)
        two = jnp.where(inner, came_two[plane, block].astype(jnp.float32), 0.0)
        top = grad[plane, block, border : 2 * border] + jnp.where(even_row, two, one)
        bottom = grad[plane, block, rows : rows + border] + jnp.where(even_row, one, two)
        return top, bottom

    for pair in range(2):
        for number, (even, odd) in enumerate(zip(ends(2 * pair, blocks), ends(2 * pair + 1, blocks))):
            right, left = join_right(even, odd, border), join_left(even, odd, border)
            span = slice(number * border, (number + 1) * border)
            side_one[pair, span] = jnp.where(even_col, right, left).astype(jnp.bfloat16)
            side_two[pair, span] = jnp.where(even_col, left, right).astype(jnp.bfloat16)
    for plane in range(4):
        for block in range(blocks):
            span = slice(block * LANES, (block + 1) * LANES)
            top, bottom = ends(plane, block)
            middle[plane, :border, span] = top
            middle[plane, border : rows - border, span] = grad[plane, block, 2 * border : rows]
            middle[plane, rows - border :, span] = bottom


def final_kernel(ncols, border, middle, mid_one, mid_two, end_one, end_two, out):
    rows, cols = middle.shape[1:]
    low = lax.broadcasted_iota(jnp.int32, (1, LANES), 1) < border
    even_col, inner = sides("col", ncols)
    parts = (
        (slice(0, border), end_one, end_two, slice(0, border)),
        (slice(border, rows - border), mid_one, mid_two, slice(0, rows - 2 * border)),
        (slice(rows - border, rows), end_one, end_two, slice(border, 2 * border)),
    )
    for span, came_one, came_two, source in parts:
        for pair in range(2):
            one = came_one[pair, source].astype(jnp.float32)
            two = jnp.where(inner, came_two[pair, source].astype(jnp.float32), 0.0)
            near = jnp.where(even_col, two, one)
            far = jnp.where(even_col, one, two)
            even, odd = 2 * pair, 2 * pair + 1
            for plane, first, last in (
                (even, near, pltpu.roll(far, border, 1)),
                (odd, pltpu.roll(near, border, 1), far),
            ):
                add_first = jnp.where(low, first, 0.0)
                add_last = jnp.where(low, 0.0, last)
                if cols == LANES:
                    out[plane, span] = middle[plane, span] + add_first + add_last
                    continue
                out[plane, span, :LANES] = middle[plane, span, :LANES] + add_first
                if cols > 2 * LANES:
                    out[plane, span, LANES : cols - LANES] = middle[plane, span, LANES : cols - LANES]
                out[plane, span, cols - LANES :] = middle[plane, span, cols - LANES :] + add_last


def local(ncols, nrows, objects, probe, amplitudes, owners, off_rows, off_cols):
    width = amplitudes.shape[-1]
    border = width // 2
    count = amplitudes.shape[2]
    rows, cols = objects.shape[2:]
    blocks = cols // LANES
    obj = objects.reshape(4, rows, cols)
    vmem = pl.BlockSpec(memory_space=pltpu.VMEM)
    anywhere = pl.BlockSpec(memory_space=pl.ANY)
    bf16 = functools.partial(jax.ShapeDtypeStruct, dtype=jnp.bfloat16)
    f32 = functools.partial(jax.ShapeDtypeStruct, dtype=jnp.float32)

    def kernel(body, ins, outs, name, scratch=(), limit=VMEM_BYTES, cost=None):
        return pl.pallas_call(
            body,
            out_shape=outs,
            in_specs=ins if isinstance(ins, list) else [vmem] * ins,
            out_specs=[vmem] * len(outs),
            scratch_shapes=list(scratch),
            compiler_params=pltpu.CompilerParams(vmem_limit_bytes=limit),
            cost_estimate=cost,
            name=name,
        )

    def across(array, way):
        return lax.ppermute(array, "col", [(i, way(i)) for i in range(ncols)])

    def swap(array, pairs):
        flat = [(a * ncols + b, c * ncols + d) for (a, b), (c, d) in pairs]
        return lax.ppermute(array, ("row", "col"), flat)

    row_one, row_two = row_partners(nrows, ncols, lambda r, c: (nrows - 1 - r, c))
    _, row_back = row_partners(nrows, ncols, lambda r, c: (r, c ^ 2))
    col_one, col_two = col_partners(nrows, ncols)
    if ncols == 8:
        ways = [functools.partial(lambda to, at: to, to) for to in range(ncols)]
    else:
        ways = routes(ncols)
    kinds = len(ways)
    line_shape = bf16((4, blocks + 1, border, LANES))
    side_shape = bf16((2, rows, LANES))

    side_one, side_two, msgs = kernel(
        functools.partial(pack_kernel, ways, ncols),
        [anywhere] * 5,
        [side_shape] * 2 + [bf16((kinds, CAP * width + NOTE, LANES))],
        "pack",
        [
            pltpu.VMEM(objects.shape, jnp.float32),
            pltpu.VMEM((count, width, width), jnp.bfloat16),
            pltpu.SMEM((3,) + owners.shape, jnp.int32),
            pltpu.SemaphoreType.DMA((5,)),
        ],
        FULL_BYTES,
    )(amplitudes, owners, off_rows, off_cols, objects)
    came_one, came_two = swap(side_one, col_one), swap(side_two, col_two)
    if ncols == 8:
        msgs = lax.all_to_all(msgs, "col", 0, 0)
    else:
        msgs = jnp.stack([across(msgs[kind], way) for kind, way in enumerate(ways)])
    side, line_one, line_two = kernel(
        functools.partial(rows_kernel, ncols, nrows),
        3,
        [bf16((4, rows, LANES))] + [line_shape] * 2,
        "rows",
        cost=HEAVY,
    )(came_one, came_two, obj)
    line_one, line_two = swap(line_one, row_one), swap(line_two, row_two)

    whole = f32((4, blocks + 1, rows + 2 * border, LANES))
    (ext,) = kernel(functools.partial(extend_kernel, nrows), 4, [whole], "extend")(
        obj, side, line_one, line_two
    )
    tables = make_tables(width)
    grad, line_one, line_two, mid_one, mid_two = kernel(
        functools.partial(main_kernel, BATCH, ncols, nrows),
        [anywhere] * 4,
        [whole] + [line_shape] * 2 + [bf16((2, rows - 2 * border, LANES))] * 2,
        "gradients",
        [
            pltpu.VMEM(tables.shape, jnp.bfloat16),
            pltpu.VMEM(probe.shape, jnp.float32),
            pltpu.VMEM(msgs.shape, jnp.bfloat16),
            pltpu.VMEM(whole.shape, jnp.float32),
            pltpu.VMEM((8, LANES), jnp.int32),
            pltpu.SMEM((8, LANES), jnp.int32),
            pltpu.SMEM((kinds * CAP + BATCH,), jnp.int32),
            pltpu.SemaphoreType.DMA((6,)),
        ],
        MAIN_BYTES,
    )(tables, probe, msgs, ext)

    line_two, line_one = swap(line_two, row_back), swap(line_one, row_one)
    mid_one, mid_two = swap(mid_one, col_one), swap(mid_two, col_two)
    middle, end_one, end_two = kernel(
        functools.partial(sides_kernel, ncols, nrows),
        3,
        [f32((4, rows, cols))] + [bf16((2, 2 * border, LANES))] * 2,
        "sides",
    )(grad, line_one, line_two)
    end_one, end_two = swap(end_one, col_one), swap(end_two, col_two)
    (out,) = kernel(
        functools.partial(final_kernel, ncols, border), 5, [f32((4, rows, cols))], "final"
    )(middle, mid_one, mid_two, end_one, end_two)
    return out.reshape(objects.shape)


def solution(mesh):
    placed = (
        P(None, None, "row", "col"),
        P(),
        P("row", "col", None, None, None),
        P("row", "col", None),
        P("row", "col", None),
        P("row", "col", None),
    )
    return jax.shard_map(
        functools.partial(local, mesh.shape["col"], mesh.shape["row"]),
        mesh=mesh,
        in_specs=placed,
        out_specs=P(None, None, "row", "col"),
        check_vma=False,
    )
```

```python
import functools
import math

import jax
import jax.numpy as jnp
import numpy as np
from jax import lax
from jax.experimental import pallas as pl
from jax.experimental.pallas import tpu as pltpu
from jax.sharding import PartitionSpec as P

FRESNEL = 24.0
REACH_OFFSETS = (-3, -2, -1, 1, 2, 3, 4)
CAP = 2
LANES = 128
NOTE = 16
FIELDS = 4
VMEM_BYTES = 40 * 1024 * 1024
FULL_BYTES = 60 * 1024 * 1024
MAIN_BYTES = 48 * 1024 * 1024
BATCH = 6
HEAVY = pl.CostEstimate(flops=10**12, bytes_accessed=10**9, transcendentals=10**9)


def make_tables(width):
    idx = np.arange(width)
    angle = (idx[:, None] * idx[None, :] % width).astype(np.float32) * np.float32(2.0 * math.pi / width)
    scale = np.float32(1.0 / math.sqrt(width))
    f_re = np.cos(angle) * scale
    f_im = -np.sin(angle) * scale
    centred = (idx + width // 2) % width - width // 2
    theta = (centred * centred).astype(np.float32) * np.float32(math.pi * FRESNEL / (width * width))
    d_re = np.cos(theta)
    d_im = -np.sin(theta)
    m_re = d_re[:, None] * f_re - d_im[:, None] * f_im
    m_im = d_re[:, None] * f_im + d_im[:, None] * f_re
    k_re = f_re @ m_re + f_im @ m_im
    k_im = f_re @ m_im - f_im @ m_re
    tables = []
    for re, im in ((k_re, k_im), (f_re, f_im)):
        tables.append(np.block([[re, -im], [im, re]]))
        tables.append(np.block([[re, im], [-im, re]]))
    return jnp.asarray(np.stack(tables).astype(jnp.bfloat16))


def row_partners(nrows, ncols, idle):
    first = [((r, c), (r ^ 1, c)) for r in range(nrows) for c in range(ncols)]
    second = []
    for r in range(nrows):
        other = ((r + 1) ^ 1) - 1
        for c in range(ncols):
            second.append(((r, c), (other, c) if 0 <= other < nrows else idle(r, c)))
    return first, second


def col_partners(nrows, ncols):
    first = [((r, c), (r, c ^ 1)) for r in range(nrows) for c in range(ncols)]
    second = []
    for c in range(ncols):
        other = ((c + 1) ^ 1) - 1
        for r in range(nrows):
            second.append(((r, c), (r, other) if 0 <= other < ncols else (r ^ 1, c)))
    return first, second


def meet(at, step, turn, size):
    odd = (at // 2 if step == 2 else at) % 2
    return (at + size + step * (1 - 2 * odd) * (1 - 2 * turn)) % size


def routes(ncols):
    paired = [
        functools.partial(lambda step, turn, at: meet(at, step, turn, ncols), step, turn)
        for step in (1, 2, 3)
        for turn in (0, 1)
    ]
    return paired + [lambda at: (at + 4) % ncols]


def sides(axis, size):
    at = lax.axis_index(axis)
    return at % 2 == 0, (at > 0) & (at < size - 1)


def join_right(even, odd, border):
    low = lax.broadcasted_iota(jnp.int32, (1, LANES), 1) < border
    return jnp.where(low, even, pltpu.roll(odd, border, 1))


def join_left(even, odd, border):
    low = lax.broadcasted_iota(jnp.int32, (1, LANES), 1) < border
    return jnp.where(low, pltpu.roll(even, border, 1), odd)


def pack_kernel(ways, ncols, amps, owners, at_rows, at_cols, obj, *refs):
    side_one, side_two, msgs, tile, packed, held, chosen, ints, sem, sent = refs
    count, width = amps.shape[2:4]
    rows, cols = obj.shape[2:]
    border = width // 2
    small = [
        pltpu.make_async_copy(ref, ints.at[number], sem.at[number])
        for number, ref in enumerate((owners, at_rows, at_cols))
    ]
    tiles = [pltpu.make_async_copy(obj.at[pair], tile.at[pair], sem.at[3 + pair]) for pair in range(2)]
    patterns = pltpu.make_async_copy(amps.at[0, 0], held, sem.at[5])
    for copy in small + [patterns] + tiles:
        copy.start()
    for copy in small + [patterns]:
        copy.wait()

    myself = lax.axis_index("col")
    lane_id = lax.broadcasted_iota(jnp.int32, (NOTE, LANES), 1)
    copies = []
    for kind, way in enumerate(ways):
        owner = way(myself)
        found = jnp.int32(0)
        slots = [jnp.int32(0)] * CAP
        for j in range(count):
            mine = ints[0, 0, 0, j] == owner
            for slot in range(CAP):
                slots[slot] = jnp.where(mine & (found == slot), j, slots[slot])
            found = found + mine.astype(jnp.int32)
        note = jnp.zeros((NOTE, LANES), jnp.float32)
        for slot in range(CAP):
            j = slots[slot]
            chosen[kind, slot * width : (slot + 1) * width] = held[j]
            live = (found > slot).astype(jnp.int32)
            for field, value in enumerate((ints[1, 0, 0, j], ints[2, 0, 0, j], live)):
                here = lane_id == slot * FIELDS + field
                note = jnp.where(here, value.astype(jnp.float32), note)
        chosen[kind, CAP * width :] = note.astype(jnp.bfloat16)
        copies.append(pltpu.make_async_copy(chosen.at[kind], msgs.at[kind], sent.at[kind]))
        copies[-1].start()

    even_col, _ = sides("col", ncols)
    for pair in range(2):
        tiles[pair].wait()
        planes = (tile.at[pair, 0], tile.at[pair, 1])
        left = join_right(*(plane[:, :LANES] for plane in planes), border)
        right = join_left(*(plane[:, cols - LANES :] for plane in planes), border)
        packed[0, pair] = jnp.where(even_col, right, left).astype(jnp.bfloat16)
        packed[1, pair] = jnp.where(even_col, left, right).astype(jnp.bfloat16)
        for number, side in enumerate((side_one, side_two)):
            at = sem.at[6 + 2 * pair + number]
            copies.append(pltpu.make_async_copy(packed.at[number, pair], side.at[pair], at))
            copies[-1].start()
    for copy in copies:
        copy.wait()


def rows_kernel(ncols, nrows, came_one, came_two, obj, side, row_one, row_two):
    rows = side.shape[1]
    border = row_two.shape[2]
    blocks = row_two.shape[1] - 1
    even_col, inner = sides("col", ncols)
    even_row, _ = sides("row", nrows)
    for pair in range(2):
        one = came_one[pair].astype(jnp.float32)
        two = jnp.where(inner, came_two[pair].astype(jnp.float32), 0.0)
        near = jnp.where(even_col, one, two)
        far = jnp.where(even_col, two, one)
        side[2 * pair] = join_right(near, far, border).astype(jnp.bfloat16)
        side[2 * pair + 1] = join_left(near, far, border).astype(jnp.bfloat16)
    low = pl.multiple_of(jnp.where(even_row, rows - border, 0), border)
    high = pl.multiple_of(jnp.where(even_row, 0, rows - border), border)
    for message, start in ((row_one, low), (row_two, high)):
        for plane in range(4):
            for block in range(blocks):
                here = obj[plane, pl.ds(start, border), block * LANES : (block + 1) * LANES]
                message[plane, block] = here.astype(jnp.bfloat16)
            message[plane, blocks] = side[plane, pl.ds(start, border), :]


def matmul(first, second):
    return jnp.dot(first, second, preferred_element_type=jnp.float32)


def each_times(fields, table):
    size = fields[0].shape[0]
    whole = matmul(jnp.concatenate(fields, axis=0), table)
    return [whole[at : at + size] for at in range(0, whole.shape[0], size)]


def quarters(field):
    half = field.shape[0] // 2
    return field[:half, :half], field[:half, half:], field[half:, :half], field[half:, half:]


def joined(a, b, c, d):
    return jnp.concatenate(
        [jnp.concatenate([a, b], axis=1), jnp.concatenate([c, d], axis=1)], axis=0
    ).astype(jnp.bfloat16)


def swapped(field):
    a, b, c, d = quarters(field)
    return joined(a, c, b, d)


def after_rows(nrows, rows, border):
    even_row, inner = sides("row", nrows)
    one = pl.multiple_of(jnp.where(even_row, border + rows, 0), border)
    two = pl.multiple_of(jnp.where(even_row, 0, border + rows), border)
    return one, two, inner


def extend_kernel(nrows, obj, side, row_one, row_two, ext):
    rows, cols = obj.shape[1:]
    border = row_one.shape[2]
    blocks = cols // LANES
    after_one, after_two, inner = after_rows(nrows, rows, border)
    for plane in range(4):
        for block in range(blocks):
            ext[plane, block, border : border + rows] = obj[plane, :, block * LANES : (block + 1) * LANES]
        ext[plane, blocks, border : border + rows] = side[plane].astype(jnp.float32)
        for block in range(blocks + 1):
            ext[plane, block, pl.ds(after_one, border), :] = row_one[plane, block].astype(jnp.float32)
            ext[plane, block, pl.ds(after_two, border), :] = jnp.where(
                inner, row_two[plane, block].astype(jnp.float32), 0.0
            )


def main_kernel(batch, ncols, nrows, *refs):
    (given_tables, given_probe, given_msgs, given_ext), refs = refs[:4], refs[4:]
    (grad, out_one, out_two, corner_two, mid_one, mid_two), refs = refs[:6], refs[6:]
    tables, probe, msgs, ext, notes, notes_s, order, sem = refs
    kinds = msgs.shape[0]
    width = probe.shape[2]
    border = width // 2
    blocks = ext.shape[1] - 1
    rows = ext.shape[2] - 2 * border
    span = (blocks + 1) * LANES

    copies = [
        pltpu.make_async_copy(
            given_msgs.at[:, pl.ds(CAP * width, NOTE)], msgs.at[:, pl.ds(CAP * width, NOTE)], sem.at[0]
        ),
        pltpu.make_async_copy(given_ext, ext, sem.at[5]),
        pltpu.make_async_copy(given_tables, tables, sem.at[1]),
        pltpu.make_async_copy(given_probe, probe, sem.at[2]),
        pltpu.make_async_copy(
            given_msgs.at[:, pl.ds(0, CAP * width)], msgs.at[:, pl.ds(0, CAP * width)], sem.at[3]
        ),
    ]
    for copy in copies:
        copy.start()
    grad[...] = jnp.zeros_like(grad)
    copies[0].wait()
    for kind in range(kinds):
        note = msgs[kind, CAP * width :].astype(jnp.float32).astype(jnp.int32)
        notes[kind : kind + 1] = note[:1]
    copy = pltpu.make_async_copy(notes, notes_s, sem.at[4])
    copy.start()
    copy.wait()
    total = jnp.int32(0)
    for kind in range(kinds):
        for slot in range(CAP):
            order[total] = kind * CAP + slot
            total = total + notes_s[kind, slot * FIELDS + 2]
    for spare in range(batch):
        order[total + spare] = 0

    lane = lax.broadcasted_iota(jnp.int32, (1, LANES), 1)

    def stages(items):
        places = []
        for number in items:
            kind, slot = order[number] // CAP, order[number] % CAP
            row = notes_s[kind, slot * FIELDS]
            col = notes_s[kind, slot * FIELDS + 1]
            start = col + (span - border)
            start = jnp.where(start >= span, start - span, start)
            first = start // LANES
            shift = start % LANES
            second = jnp.where(first == blocks, 0, first + 1)
            places.append((kind, slot, row, first, second, shift))
        windows = []
        for _, _, row, first, second, shift in places:
            window = []
            for plane in range(4):
                a = ext[plane, first, pl.ds(row, width), :]
                b = ext[plane, second, pl.ds(row, width), :]
                both = jnp.where(lane >= shift, a, b)
                window.append(pltpu.roll(both, (LANES - shift) % LANES, 1))
            windows.append(window)
        fields = []
        for window in windows:
            parts = []
            for mode in range(2):
                p_re, p_im = probe[mode, 0], probe[mode, 1]
                parts.append((p_re * window[0] - p_im * window[1], p_re * window[1] + p_im * window[0]))
            fields.append(joined(parts[0][0], parts[1][0], parts[0][1], parts[1][1]))
        fields = [swapped(matmul(tables[0], f)) for f in fields]
        phis = each_times(fields, tables[1])
        fields = []
        for window, phi in zip(windows, phis):
            a_re, a_im, b_re, b_im = quarters(phi)
            w_re, w_im = window[2], window[3]
            fields.append(
                joined(
                    a_re * w_re - a_im * w_im,
                    b_re * w_re - b_im * w_im,
                    a_re * w_im + a_im * w_re,
                    b_re * w_im + b_im * w_re,
                )
            )
        fields = [swapped(matmul(tables[2], f)) for f in fields]
        fars = each_times(fields, tables[3])
        fields = []
        for place, far in zip(places, fars):
            a_re, a_im, b_re, b_im = quarters(far)
            inten = a_re * a_re + a_im * a_im + b_re * b_re + b_im * b_im
            kind, slot = place[:2]
            amp = msgs[kind, pl.ds(pl.multiple_of(slot * width, width), width), :].astype(jnp.float32)
            keep = 1.0 - amp * lax.rsqrt(jnp.maximum(inten, 1.0))
            fields.append(joined(a_re * keep, b_re * keep, a_im * keep, b_im * keep))
        fields = [swapped(matmul(tables[3], f)) for f in fields]
        seconds = each_times(fields, tables[2])
        fields = []
        for window, second in zip(windows, seconds):
            a_re, a_im, b_re, b_im = quarters(second)
            w_re, w_im = window[2], window[3]
            fields.append(
                joined(
                    w_re * a_re + w_im * a_im,
                    w_re * b_re + w_im * b_im,
                    w_re * a_im - w_im * a_re,
                    w_re * b_im - w_im * b_re,
                )
            )
        fields = [swapped(matmul(tables[1], f)) for f in fields]
        firsts = each_times(fields, tables[0])
        for number, place, phi, one, two in zip(items, places, phis, firsts, seconds):
            _, _, row, first, second, shift = place
            sums = []
            probes = (probe[0, 0], probe[0, 1], probe[1, 0], probe[1, 1])
            for left, right in ((probes, one), (quarters(phi), two)):
                p_re, p_im, q_re, q_im = left
                a_re, a_im, b_re, b_im = quarters(right)
                sums.append(p_re * a_re + p_im * a_im + q_re * b_re + q_im * b_im)
                sums.append(p_re * a_im - p_im * a_re + q_re * b_im - q_im * b_re)
            live = number < total
            for plane in range(4):
                moved = pltpu.roll(sums[plane], shift, 1)
                grad[plane, first, pl.ds(row, width), :] += jnp.where((lane >= shift) & live, moved, 0.0)
                grad[plane, second, pl.ds(row, width), :] += jnp.where((lane < shift) & live, moved, 0.0)

    def visit(step, carry):
        stages([batch * step + item for item in range(batch)])
        return carry

    for copy in copies[1:]:
        copy.wait()
    lax.fori_loop(0, (total + batch - 1) // batch, visit, 0)

    after_one, after_two, _ = after_rows(nrows, rows, border)
    for plane in range(4):
        for block in range(blocks + 1):
            out_one[plane, block] = grad[plane, block, pl.ds(after_one, border), :].astype(jnp.bfloat16)
            two = grad[plane, block, pl.ds(after_two, border), :].astype(jnp.bfloat16)
            if block < blocks:
                out_two[plane, block] = two
            else:
                corner_two[plane] = two
    even_col, _ = sides("col", ncols)
    middle = slice(2 * border, rows)
    for pair in range(2):
        even, odd = grad[2 * pair, blocks, middle], grad[2 * pair + 1, blocks, middle]
        right, left = join_right(even, odd, border), join_left(even, odd, border)
        mid_one[pair] = jnp.where(even_col, right, left).astype(jnp.bfloat16)
        mid_two[pair] = jnp.where(even_col, left, right).astype(jnp.bfloat16)


def ends(even_row, inner, one, two):
    one = one.astype(jnp.float32)
    two = jnp.where(inner, two.astype(jnp.float32), 0.0)
    return jnp.where(even_row, two, one), jnp.where(even_row, one, two)


def sides_kernel(ncols, nrows, grad, row_one, corner_two, side_one, side_two):
    blocks = row_one.shape[1] - 1
    border = row_one.shape[2]
    rows = grad.shape[2] - 2 * border
    even_col, _ = sides("col", ncols)
    even_row, inner = sides("row", nrows)
    for pair in range(2):
        planes = (2 * pair, 2 * pair + 1)
        came = [ends(even_row, inner, row_one[plane, blocks], corner_two[plane]) for plane in planes]
        for number, at in enumerate((border, rows)):
            even, odd = (
                grad[plane, blocks, at : at + border] + here[number] for plane, here in zip(planes, came)
            )
            right, left = join_right(even, odd, border), join_left(even, odd, border)
            span = slice(number * border, (number + 1) * border)
            side_one[pair, span] = jnp.where(even_col, right, left).astype(jnp.bfloat16)
            side_two[pair, span] = jnp.where(even_col, left, right).astype(jnp.bfloat16)


def final_kernel(ncols, nrows, grad, row_one, row_two, mid_one, mid_two, end_one, end_two, out, whole, sem):
    blocks, border = row_two.shape[1:3]
    rows = grad.shape[2] - 2 * border
    low = lax.broadcasted_iota(jnp.int32, (1, LANES), 1) < border
    even_col, inner_col = sides("col", ncols)
    even_row, inner_row = sides("row", nrows)
    copies = []
    for pair in range(2):
        near, far = [], []
        for came_one, came_two in ((mid_one, mid_two), (end_one, end_two)):
            one = came_one[pair].astype(jnp.float32)
            two = jnp.where(inner_col, came_two[pair].astype(jnp.float32), 0.0)
            near.append(jnp.where(even_col, two, one))
            far.append(jnp.where(even_col, one, two))
        near, far = (
            jnp.concatenate([end[:border], mid, end[border:]], axis=0) for mid, end in (near, far)
        )
        for plane, first, last in (
            (2 * pair, near, pltpu.roll(far, border, 1)),
            (2 * pair + 1, pltpu.roll(near, border, 1), far),
        ):
            for block in range(blocks):
                span = slice(block * LANES, (block + 1) * LANES)
                total = grad[plane, block, border : border + rows]
                if block == 0:
                    total = total + jnp.where(low, first, 0.0)
                if block == blocks - 1:
                    total = total + jnp.where(low, 0.0, last)
                top, bottom = ends(even_row, inner_row, row_one[plane, block], row_two[plane, block])
                whole[plane, :border, span] = total[:border] + top
                whole[plane, border : rows - border, span] = total[border : rows - border]
                whole[plane, rows - border :, span] = total[rows - border :] + bottom
            copies.append(pltpu.make_async_copy(whole.at[plane], out.at[plane], sem.at[plane]))
            copies[-1].start()
    for copy in copies:
        copy.wait()


def local(ncols, nrows, objects, probe, amplitudes, owners, off_rows, off_cols):
    width = amplitudes.shape[-1]
    border = width // 2
    count = amplitudes.shape[2]
    rows, cols = objects.shape[2:]
    blocks = cols // LANES
    obj = objects.reshape(4, rows, cols)
    vmem = pl.BlockSpec(memory_space=pltpu.VMEM)
    anywhere = pl.BlockSpec(memory_space=pl.ANY)
    bf16 = functools.partial(jax.ShapeDtypeStruct, dtype=jnp.bfloat16)
    f32 = functools.partial(jax.ShapeDtypeStruct, dtype=jnp.float32)

    def kernel(body, ins, outs, name, scratch=(), limit=VMEM_BYTES, cost=None, to=vmem):
        return pl.pallas_call(
            body,
            out_shape=outs,
            in_specs=ins if isinstance(ins, list) else [vmem] * ins,
            out_specs=[to] * len(outs),
            scratch_shapes=list(scratch),
            compiler_params=pltpu.CompilerParams(vmem_limit_bytes=limit),
            cost_estimate=cost,
            name=name,
        )

    def across(array, way):
        return lax.ppermute(array, "col", [(i, way(i)) for i in range(ncols)])

    def swap(array, pairs):
        flat = [(a * ncols + b, c * ncols + d) for (a, b), (c, d) in pairs]
        return lax.ppermute(array, ("row", "col"), flat)

    row_one, row_two = row_partners(nrows, ncols, lambda r, c: (nrows - 1 - r, c))
    _, row_back = row_partners(nrows, ncols, lambda r, c: (r, c ^ 2))
    col_one, col_two = col_partners(nrows, ncols)
    if ncols == 8:
        ways = [functools.partial(lambda to, at: to, to) for to in range(ncols)]
    else:
        ways = routes(ncols)
    kinds = len(ways)
    line_shape = bf16((4, blocks + 1, border, LANES))
    side_shape = bf16((2, rows, LANES))

    side_one, side_two, msgs = kernel(
        functools.partial(pack_kernel, ways, ncols),
        [anywhere] * 5,
        [side_shape] * 2 + [bf16((kinds, CAP * width + NOTE, LANES))],
        "pack",
        [
            pltpu.VMEM(objects.shape, jnp.float32),
            pltpu.VMEM((2,) + side_shape.shape, jnp.bfloat16),
            pltpu.VMEM((count, width, width), jnp.bfloat16),
            pltpu.VMEM((kinds, CAP * width + NOTE, LANES), jnp.bfloat16),
            pltpu.SMEM((3,) + owners.shape, jnp.int32),
            pltpu.SemaphoreType.DMA((10,)),
            pltpu.SemaphoreType.DMA((kinds,)),
        ],
        FULL_BYTES,
        to=anywhere,
    )(amplitudes, owners, off_rows, off_cols, objects)
    came_one, came_two = swap(side_one, col_one), swap(side_two, col_two)
    if ncols == 8:
        msgs = lax.all_to_all(msgs, "col", 0, 0)
    else:
        msgs = jnp.stack([across(msgs[kind], way) for kind, way in enumerate(ways)])
    side, line_one, line_two = kernel(
        functools.partial(rows_kernel, ncols, nrows),
        3,
        [bf16((4, rows, LANES))] + [line_shape] * 2,
        "rows",
        cost=HEAVY,
    )(came_one, came_two, obj)
    line_one, line_two = swap(line_one, row_one), swap(line_two, row_two)

    whole = f32((4, blocks + 1, rows + 2 * border, LANES))
    (ext,) = kernel(functools.partial(extend_kernel, nrows), 4, [whole], "extend")(
        obj, side, line_one, line_two
    )
    tables = make_tables(width)
    edge_shape = bf16((4, blocks, border, LANES))
    corner_shape = bf16((4, border, LANES))
    grad, line_one, edge_two, corner_two, mid_one, mid_two = kernel(
        functools.partial(main_kernel, BATCH, ncols, nrows),
        [anywhere] * 4,
        [whole, line_shape, edge_shape, corner_shape] + [bf16((2, rows - 2 * border, LANES))] * 2,
        "gradients",
        [
            pltpu.VMEM(tables.shape, jnp.bfloat16),
            pltpu.VMEM(probe.shape, jnp.float32),
            pltpu.VMEM(msgs.shape, jnp.bfloat16),
            pltpu.VMEM(whole.shape, jnp.float32),
            pltpu.VMEM((8, LANES), jnp.int32),
            pltpu.SMEM((8, LANES), jnp.int32),
            pltpu.SMEM((kinds * CAP + BATCH,), jnp.int32),
            pltpu.SemaphoreType.DMA((6,)),
        ],
        MAIN_BYTES,
    )(tables, probe, msgs, ext)

    corner_two, line_one = swap(corner_two, row_back), swap(line_one, row_one)
    mid_one, mid_two = swap(mid_one, col_one), swap(mid_two, col_two)
    edge_two = swap(edge_two, row_back)
    end_one, end_two = kernel(
        functools.partial(sides_kernel, ncols, nrows), 3, [bf16((2, 2 * border, LANES))] * 2, "sides", cost=pl.CostEstimate(flops=10**10, bytes_accessed=10**6, transcendentals=0)
    )(grad, line_one, corner_two)
    end_one, end_two = swap(end_one, col_one), swap(end_two, col_two)
    (out,) = kernel(
        functools.partial(final_kernel, ncols, nrows),
        7,
        [f32((4, rows, cols))],
        "final",
        [pltpu.VMEM((4, rows, cols), jnp.float32), pltpu.SemaphoreType.DMA((4,))],
        to=anywhere,
    )(grad, line_one, edge_two, mid_one, mid_two, end_one, end_two)
    return out.reshape(objects.shape)


def solution(mesh):
    placed = (
        P(None, None, "row", "col"),
        P(),
        P("row", "col", None, None, None),
        P("row", "col", None),
        P("row", "col", None),
        P("row", "col", None),
    )
    return jax.shard_map(
        functools.partial(local, mesh.shape["col"], mesh.shape["row"]),
        mesh=mesh,
        in_specs=placed,
        out_specs=P(None, None, "row", "col"),
        check_vma=False,
    )
```

```python
import functools
import math

import jax
import jax.numpy as jnp
import numpy as np
from jax import lax
from jax.experimental import pallas as pl
from jax.experimental.pallas import tpu as pltpu
from jax.sharding import PartitionSpec as P

FRESNEL = 24.0
REACH_OFFSETS = (-3, -2, -1, 1, 2, 3, 4)
CAP = 2
LANES = 128
NOTE = 16
FIELDS = 4
VMEM_BYTES = 40 * 1024 * 1024
FULL_BYTES = 60 * 1024 * 1024
MAIN_BYTES = 48 * 1024 * 1024
BATCH = 6
HEAVY = pl.CostEstimate(flops=10**12, bytes_accessed=10**9, transcendentals=10**9)


def make_tables(width):
    idx = np.arange(width)
    angle = (idx[:, None] * idx[None, :] % width).astype(np.float32) * np.float32(2.0 * math.pi / width)
    scale = np.float32(1.0 / math.sqrt(width))
    f_re = np.cos(angle) * scale
    f_im = -np.sin(angle) * scale
    centred = (idx + width // 2) % width - width // 2
    theta = (centred * centred).astype(np.float32) * np.float32(math.pi * FRESNEL / (width * width))
    d_re = np.cos(theta)
    d_im = -np.sin(theta)
    m_re = d_re[:, None] * f_re - d_im[:, None] * f_im
    m_im = d_re[:, None] * f_im + d_im[:, None] * f_re
    k_re = f_re @ m_re + f_im @ m_im
    k_im = f_re @ m_im - f_im @ m_re
    tables = []
    for re, im in ((k_re, k_im), (f_re, f_im)):
        tables.append(np.block([[re, -im], [im, re]]))
        tables.append(np.block([[re, im], [-im, re]]))
    return jnp.asarray(np.stack(tables).astype(jnp.bfloat16))


def row_partners(nrows, ncols, idle):
    first = [((r, c), (r ^ 1, c)) for r in range(nrows) for c in range(ncols)]
    second = []
    for r in range(nrows):
        other = ((r + 1) ^ 1) - 1
        for c in range(ncols):
            second.append(((r, c), (other, c) if 0 <= other < nrows else idle(r, c)))
    return first, second


def col_partners(nrows, ncols):
    first = [((r, c), (r, c ^ 1)) for r in range(nrows) for c in range(ncols)]
    second = []
    for c in range(ncols):
        other = ((c + 1) ^ 1) - 1
        for r in range(nrows):
            second.append(((r, c), (r, other) if 0 <= other < ncols else (r ^ 1, c)))
    return first, second


def meet(at, step, turn, size):
    odd = (at // 2 if step == 2 else at) % 2
    return (at + size + step * (1 - 2 * odd) * (1 - 2 * turn)) % size


def routes(ncols):
    paired = [
        functools.partial(lambda step, turn, at: meet(at, step, turn, ncols), step, turn)
        for step in (1, 2, 3)
        for turn in (0, 1)
    ]
    return paired + [lambda at: (at + 4) % ncols]


def sides(axis, size):
    at = lax.axis_index(axis)
    return at % 2 == 0, (at > 0) & (at < size - 1)


def join_right(even, odd, border):
    low = lax.broadcasted_iota(jnp.int32, (1, LANES), 1) < border
    return jnp.where(low, even, pltpu.roll(odd, border, 1))


def join_left(even, odd, border):
    low = lax.broadcasted_iota(jnp.int32, (1, LANES), 1) < border
    return jnp.where(low, pltpu.roll(even, border, 1), odd)


def pack_kernel(ways, ncols, amps, owners, at_rows, at_cols, obj, *refs):
    side_one, side_two, msgs, tile, packed, held, chosen, ints, sem, sent = refs
    count, width = amps.shape[2:4]
    rows, cols = obj.shape[2:]
    border = width // 2
    small = [
        pltpu.make_async_copy(ref, ints.at[number], sem.at[number])
        for number, ref in enumerate((owners, at_rows, at_cols))
    ]
    tiles = [pltpu.make_async_copy(obj.at[pair], tile.at[pair], sem.at[3 + pair]) for pair in range(2)]
    patterns = pltpu.make_async_copy(amps.at[0, 0], held, sem.at[5])
    for copy in small + [patterns] + tiles:
        copy.start()
    for copy in small + [patterns]:
        copy.wait()

    myself = lax.axis_index("col")
    lane_id = lax.broadcasted_iota(jnp.int32, (NOTE, LANES), 1)
    copies = []
    for kind, way in enumerate(ways):
        owner = way(myself)
        found = jnp.int32(0)
        slots = [jnp.int32(0)] * CAP
        for j in range(count):
            mine = ints[0, 0, 0, j] == owner
            for slot in range(CAP):
                slots[slot] = jnp.where(mine & (found == slot), j, slots[slot])
            found = found + mine.astype(jnp.int32)
        note = jnp.zeros((NOTE, LANES), jnp.float32)
        for slot in range(CAP):
            j = slots[slot]
            chosen[kind, slot * width : (slot + 1) * width] = held[j]
            live = (found > slot).astype(jnp.int32)
            for field, value in enumerate((ints[1, 0, 0, j], ints[2, 0, 0, j], live)):
                here = lane_id == slot * FIELDS + field
                note = jnp.where(here, value.astype(jnp.float32), note)
        chosen[kind, CAP * width :] = note.astype(jnp.bfloat16)
        copies.append(pltpu.make_async_copy(chosen.at[kind], msgs.at[kind], sent.at[kind]))
        copies[-1].start()

    even_col, _ = sides("col", ncols)
    for pair in range(2):
        tiles[pair].wait()
        planes = (tile.at[pair, 0], tile.at[pair, 1])
        left = join_right(*(plane[:, :LANES] for plane in planes), border)
        right = join_left(*(plane[:, cols - LANES :] for plane in planes), border)
        packed[0, pair] = jnp.where(even_col, right, left).astype(jnp.bfloat16)
        packed[1, pair] = jnp.where(even_col, left, right).astype(jnp.bfloat16)
        for number, side in enumerate((side_one, side_two)):
            at = sem.at[6 + 2 * pair + number]
            copies.append(pltpu.make_async_copy(packed.at[number, pair], side.at[pair], at))
            copies[-1].start()
    for copy in copies:
        copy.wait()


def rows_kernel(ncols, nrows, came_one, came_two, obj, side, row_one, row_two):
    rows = side.shape[1]
    border = row_two.shape[2]
    blocks = row_two.shape[1] - 1
    even_col, inner = sides("col", ncols)
    even_row, _ = sides("row", nrows)
    for pair in range(2):
        one = came_one[pair].astype(jnp.float32)
        two = jnp.where(inner, came_two[pair].astype(jnp.float32), 0.0)
        near = jnp.where(even_col, one, two)
        far = jnp.where(even_col, two, one)
        side[2 * pair] = join_right(near, far, border).astype(jnp.bfloat16)
        side[2 * pair + 1] = join_left(near, far, border).astype(jnp.bfloat16)
    low = pl.multiple_of(jnp.where(even_row, rows - border, 0), border)
    high = pl.multiple_of(jnp.where(even_row, 0, rows - border), border)
    for message, start in ((row_one, low), (row_two, high)):
        for plane in range(4):
            for block in range(blocks):
                here = obj[plane, pl.ds(start, border), block * LANES : (block + 1) * LANES]
                message[plane, block] = here.astype(jnp.bfloat16)
            message[plane, blocks] = side[plane, pl.ds(start, border), :]


def matmul(first, second):
    return jnp.dot(first, second, preferred_element_type=jnp.float32)


def each_times(fields, table):
    size = fields[0].shape[0]
    whole = matmul(jnp.concatenate(fields, axis=0), table)
    return [whole[at : at + size] for at in range(0, whole.shape[0], size)]


def quarters(field):
    half = field.shape[0] // 2
    return field[:half, :half], field[:half, half:], field[half:, :half], field[half:, half:]


def joined(a, b, c, d):
    return jnp.concatenate(
        [jnp.concatenate([a, b], axis=1), jnp.concatenate([c, d], axis=1)], axis=0
    ).astype(jnp.bfloat16)


def swapped(field):
    a, b, c, d = quarters(field)
    return joined(a, c, b, d)


def after_rows(nrows, rows, border):
    even_row, inner = sides("row", nrows)
    one = pl.multiple_of(jnp.where(even_row, border + rows, 0), border)
    two = pl.multiple_of(jnp.where(even_row, 0, border + rows), border)
    return one, two, inner


def extend_kernel(nrows, obj, side, row_one, row_two, ext):
    rows, cols = obj.shape[1:]
    border = row_one.shape[2]
    blocks = cols // LANES
    after_one, after_two, inner = after_rows(nrows, rows, border)
    for plane in range(4):
        for block in range(blocks):
            ext[plane, block, border : border + rows] = obj[plane, :, block * LANES : (block + 1) * LANES]
        ext[plane, blocks, border : border + rows] = side[plane].astype(jnp.float32)
        for block in range(blocks + 1):
            ext[plane, block, pl.ds(after_one, border), :] = row_one[plane, block].astype(jnp.float32)
            ext[plane, block, pl.ds(after_two, border), :] = jnp.where(
                inner, row_two[plane, block].astype(jnp.float32), 0.0
            )


def main_kernel(batch, ncols, nrows, *refs):
    (given_tables, given_probe, given_msgs, given_ext), refs = refs[:4], refs[4:]
    (grad, out_one, out_two, corner_two, mid_one, mid_two), refs = refs[:6], refs[6:]
    tables, probe, msgs, ext, notes, notes_s, order, sem = refs
    kinds = msgs.shape[0]
    width = probe.shape[2]
    border = width // 2
    blocks = ext.shape[1] - 1
    rows = ext.shape[2] - 2 * border
    span = (blocks + 1) * LANES

    copies = [
        pltpu.make_async_copy(
            given_msgs.at[:, pl.ds(CAP * width, NOTE)], msgs.at[:, pl.ds(CAP * width, NOTE)], sem.at[0]
        ),
        pltpu.make_async_copy(given_ext, ext, sem.at[5]),
        pltpu.make_async_copy(given_tables, tables, sem.at[1]),
        pltpu.make_async_copy(given_probe, probe, sem.at[2]),
        pltpu.make_async_copy(
            given_msgs.at[:, pl.ds(0, CAP * width)], msgs.at[:, pl.ds(0, CAP * width)], sem.at[3]
        ),
    ]
    for copy in copies:
        copy.start()
    grad[...] = jnp.zeros_like(grad)
    copies[0].wait()
    for kind in range(kinds):
        note = msgs[kind, CAP * width :].astype(jnp.float32).astype(jnp.int32)
        notes[kind : kind + 1] = note[:1]
    copy = pltpu.make_async_copy(notes, notes_s, sem.at[4])
    copy.start()
    copy.wait()
    total = jnp.int32(0)
    for kind in range(kinds):
        for slot in range(CAP):
            order[total] = kind * CAP + slot
            total = total + notes_s[kind, slot * FIELDS + 2]
    for spare in range(batch):
        order[total + spare] = 0

    lane = lax.broadcasted_iota(jnp.int32, (1, LANES), 1)

    def stages(items):
        places = []
        for number in items:
            kind, slot = order[number] // CAP, order[number] % CAP
            row = notes_s[kind, slot * FIELDS]
            col = notes_s[kind, slot * FIELDS + 1]
            start = col + (span - border)
            start = jnp.where(start >= span, start - span, start)
            first = start // LANES
            shift = start % LANES
            second = jnp.where(first == blocks, 0, first + 1)
            places.append((kind, slot, row, first, second, shift))
        windows = []
        for _, _, row, first, second, shift in places:
            window = []
            for plane in range(4):
                a = ext[plane, first, pl.ds(row, width), :]
                b = ext[plane, second, pl.ds(row, width), :]
                both = jnp.where(lane >= shift, a, b)
                window.append(pltpu.roll(both, (LANES - shift) % LANES, 1))
            windows.append(window)
        fields = []
        for window in windows:
            parts = []
            for mode in range(2):
                p_re, p_im = probe[mode, 0], probe[mode, 1]
                parts.append((p_re * window[0] - p_im * window[1], p_re * window[1] + p_im * window[0]))
            fields.append(joined(parts[0][0], parts[1][0], parts[0][1], parts[1][1]))
        fields = [swapped(matmul(tables[0], f)) for f in fields]
        phis = each_times(fields, tables[1])
        fields = []
        for window, phi in zip(windows, phis):
            a_re, a_im, b_re, b_im = quarters(phi)
            w_re, w_im = window[2], window[3]
            fields.append(
                joined(
                    a_re * w_re - a_im * w_im,
                    b_re * w_re - b_im * w_im,
                    a_re * w_im + a_im * w_re,
                    b_re * w_im + b_im * w_re,
                )
            )
        fields = [swapped(matmul(tables[2], f)) for f in fields]
        fars = each_times(fields, tables[3])
        fields = []
        for place, far in zip(places, fars):
            a_re, a_im, b_re, b_im = quarters(far)
            inten = a_re * a_re + a_im * a_im + b_re * b_re + b_im * b_im
            kind, slot = place[:2]
            amp = msgs[kind, pl.ds(pl.multiple_of(slot * width, width), width), :].astype(jnp.float32)
            keep = 1.0 - amp * lax.rsqrt(jnp.maximum(inten, 1.0))
            fields.append(joined(a_re * keep, b_re * keep, a_im * keep, b_im * keep))
        fields = [swapped(matmul(tables[3], f)) for f in fields]
        seconds = each_times(fields, tables[2])
        fields = []
        for window, second in zip(windows, seconds):
            a_re, a_im, b_re, b_im = quarters(second)
            w_re, w_im = window[2], window[3]
            fields.append(
                joined(
                    w_re * a_re + w_im * a_im,
                    w_re * b_re + w_im * b_im,
                    w_re * a_im - w_im * a_re,
                    w_re * b_im - w_im * b_re,
                )
            )
        fields = [swapped(matmul(tables[1], f)) for f in fields]
        firsts = each_times(fields, tables[0])
        for number, place, phi, one, two in zip(items, places, phis, firsts, seconds):
            _, _, row, first, second, shift = place
            sums = []
            probes = (probe[0, 0], probe[0, 1], probe[1, 0], probe[1, 1])
            for left, right in ((probes, one), (quarters(phi), two)):
                p_re, p_im, q_re, q_im = left
                a_re, a_im, b_re, b_im = quarters(right)
                sums.append(p_re * a_re + p_im * a_im + q_re * b_re + q_im * b_im)
                sums.append(p_re * a_im - p_im * a_re + q_re * b_im - q_im * b_re)
            live = number < total
            for plane in range(4):
                moved = pltpu.roll(sums[plane], shift, 1)
                grad[plane, first, pl.ds(row, width), :] += jnp.where((lane >= shift) & live, moved, 0.0)
                grad[plane, second, pl.ds(row, width), :] += jnp.where((lane < shift) & live, moved, 0.0)

    def visit(step, carry):
        stages([batch * step + item for item in range(batch)])
        return carry

    for copy in copies[1:]:
        copy.wait()
    lax.fori_loop(0, (total + batch - 1) // batch, visit, 0)

    after_one, after_two, _ = after_rows(nrows, rows, border)
    for plane in range(4):
        for block in range(blocks + 1):
            out_one[plane, block] = grad[plane, block, pl.ds(after_one, border), :].astype(jnp.bfloat16)
            two = grad[plane, block, pl.ds(after_two, border), :].astype(jnp.bfloat16)
            if block < blocks:
                out_two[plane, block] = two
            else:
                corner_two[plane] = two
    even_col, _ = sides("col", ncols)
    middle = slice(2 * border, rows)
    for pair in range(2):
        even, odd = grad[2 * pair, blocks, middle], grad[2 * pair + 1, blocks, middle]
        right, left = join_right(even, odd, border), join_left(even, odd, border)
        mid_one[pair] = jnp.where(even_col, right, left).astype(jnp.bfloat16)
        mid_two[pair] = jnp.where(even_col, left, right).astype(jnp.bfloat16)


def ends(even_row, inner, one, two):
    one = one.astype(jnp.float32)
    two = jnp.where(inner, two.astype(jnp.float32), 0.0)
    return jnp.where(even_row, two, one), jnp.where(even_row, one, two)


def sides_kernel(ncols, nrows, grad, row_one, corner_two, side_one, side_two):
    blocks = row_one.shape[1] - 1
    border = row_one.shape[2]
    rows = grad.shape[2] - 2 * border
    even_col, _ = sides("col", ncols)
    even_row, inner = sides("row", nrows)
    for pair in range(2):
        planes = (2 * pair, 2 * pair + 1)
        came = [ends(even_row, inner, row_one[plane, blocks], corner_two[plane]) for plane in planes]
        for number, at in enumerate((border, rows)):
            even, odd = (
                grad[plane, blocks, at : at + border] + here[number] for plane, here in zip(planes, came)
            )
            right, left = join_right(even, odd, border), join_left(even, odd, border)
            span = slice(number * border, (number + 1) * border)
            side_one[pair, span] = jnp.where(even_col, right, left).astype(jnp.bfloat16)
            side_two[pair, span] = jnp.where(even_col, left, right).astype(jnp.bfloat16)


def column_sums(ncols, border, came_one, came_two, pair):
    low = lax.broadcasted_iota(jnp.int32, (1, LANES), 1) < border
    even_col, inner = sides("col", ncols)
    one = came_one[pair].astype(jnp.float32)
    two = jnp.where(inner, came_two[pair].astype(jnp.float32), 0.0)
    near, far = jnp.where(even_col, two, one), jnp.where(even_col, one, two)
    return (
        (jnp.where(low, near, 0.0), jnp.where(low, 0.0, pltpu.roll(far, border, 1))),
        (jnp.where(low, pltpu.roll(near, border, 1), 0.0), jnp.where(low, 0.0, far)),
    )


def middle_kernel(ncols, grad, mid_one, mid_two, out, whole, sem):
    height, cols = whole.shape[1:]
    border = (out.shape[1] - height) // 2
    blocks = cols // LANES
    copies = []
    for pair in range(2):
        for odd, (first, last) in enumerate(column_sums(ncols, border, mid_one, mid_two, pair)):
            plane = 2 * pair + odd
            for block in range(blocks):
                total = grad[plane, block, 2 * border : 2 * border + height]
                if block == 0:
                    total = total + first
                if block == blocks - 1:
                    total = total + last
                whole[plane, :, block * LANES : (block + 1) * LANES] = total
            span = pl.ds(border, height)
            copies.append(pltpu.make_async_copy(whole.at[plane], out.at[plane, span], sem.at[plane]))
            copies[-1].start()
    for copy in copies:
        copy.wait()


def final_kernel(ncols, nrows, grad, row_one, row_two, end_one, end_two, begun, out, whole, sem):
    blocks, border = row_two.shape[1:3]
    rows = grad.shape[2] - 2 * border
    even_row, inner = sides("row", nrows)
    copies = []
    for pair in range(2):
        for odd, (first, last) in enumerate(column_sums(ncols, border, end_one, end_two, pair)):
            plane = 2 * pair + odd
            for block in range(blocks):
                came = ends(even_row, inner, row_one[plane, block], row_two[plane, block])
                for number, at in enumerate((border, rows)):
                    span = slice(number * border, (number + 1) * border)
                    total = grad[plane, block, at : at + border] + came[number]
                    if block == 0:
                        total = total + first[span]
                    if block == blocks - 1:
                        total = total + last[span]
                    whole[plane, span, block * LANES : (block + 1) * LANES] = total
            for number, at in enumerate((0, rows - border)):
                source = whole.at[plane, pl.ds(number * border, border)]
                copies.append(
                    pltpu.make_async_copy(source, out.at[plane, pl.ds(at, border)], sem.at[plane, number])
                )
                copies[-1].start()
    for copy in copies:
        copy.wait()


def local(ncols, nrows, objects, probe, amplitudes, owners, off_rows, off_cols):
    width = amplitudes.shape[-1]
    border = width // 2
    count = amplitudes.shape[2]
    rows, cols = objects.shape[2:]
    blocks = cols // LANES
    obj = objects.reshape(4, rows, cols)
    vmem = pl.BlockSpec(memory_space=pltpu.VMEM)
    anywhere = pl.BlockSpec(memory_space=pl.ANY)
    bf16 = functools.partial(jax.ShapeDtypeStruct, dtype=jnp.bfloat16)
    f32 = functools.partial(jax.ShapeDtypeStruct, dtype=jnp.float32)

    def kernel(body, ins, outs, name, scratch=(), limit=VMEM_BYTES, cost=None, to=vmem, alias={}):
        return pl.pallas_call(
            body,
            out_shape=outs,
            in_specs=ins if isinstance(ins, list) else [vmem] * ins,
            out_specs=[to] * len(outs),
            scratch_shapes=list(scratch),
            compiler_params=pltpu.CompilerParams(vmem_limit_bytes=limit),
            cost_estimate=cost,
            input_output_aliases=alias,
            name=name,
        )

    def across(array, way):
        return lax.ppermute(array, "col", [(i, way(i)) for i in range(ncols)])

    def swap(array, pairs):
        flat = [(a * ncols + b, c * ncols + d) for (a, b), (c, d) in pairs]
        return lax.ppermute(array, ("row", "col"), flat)

    row_one, row_two = row_partners(nrows, ncols, lambda r, c: (nrows - 1 - r, c))
    col_one, col_two = col_partners(nrows, ncols)
    if ncols == 8:
        ways = [functools.partial(lambda to, at: to, to) for to in range(ncols)]
    else:
        ways = routes(ncols)
    kinds = len(ways)
    line_shape = bf16((4, blocks + 1, border, LANES))
    side_shape = bf16((2, rows, LANES))

    side_one, side_two, msgs = kernel(
        functools.partial(pack_kernel, ways, ncols),
        [anywhere] * 5,
        [side_shape] * 2 + [bf16((kinds, CAP * width + NOTE, LANES))],
        "pack",
        [
            pltpu.VMEM(objects.shape, jnp.float32),
            pltpu.VMEM((2,) + side_shape.shape, jnp.bfloat16),
            pltpu.VMEM((count, width, width), jnp.bfloat16),
            pltpu.VMEM((kinds, CAP * width + NOTE, LANES), jnp.bfloat16),
            pltpu.SMEM((3,) + owners.shape, jnp.int32),
            pltpu.SemaphoreType.DMA((10,)),
            pltpu.SemaphoreType.DMA((kinds,)),
        ],
        FULL_BYTES,
        to=anywhere,
    )(amplitudes, owners, off_rows, off_cols, objects)
    came_one, came_two = swap(side_one, col_one), swap(side_two, col_two)
    if ncols == 8:
        msgs = lax.all_to_all(msgs, "col", 0, 0)
    else:
        msgs = jnp.stack([across(msgs[kind], way) for kind, way in enumerate(ways)])
    side, line_one, line_two = kernel(
        functools.partial(rows_kernel, ncols, nrows),
        3,
        [bf16((4, rows, LANES))] + [line_shape] * 2,
        "rows",
        cost=HEAVY,
    )(came_one, came_two, obj)
    line_one, line_two = swap(line_one, row_one), swap(line_two, row_two)

    whole = f32((4, blocks + 1, rows + 2 * border, LANES))
    (ext,) = kernel(functools.partial(extend_kernel, nrows), 4, [whole], "extend")(
        obj, side, line_one, line_two
    )
    tables = make_tables(width)
    edge_shape = bf16((4, blocks, border, LANES))
    corner_shape = bf16((4, border, LANES))
    grad, line_one, edge_two, corner_two, mid_one, mid_two = kernel(
        functools.partial(main_kernel, BATCH, ncols, nrows),
        [anywhere] * 4,
        [whole, line_shape, edge_shape, corner_shape] + [bf16((2, rows - 2 * border, LANES))] * 2,
        "gradients",
        [
            pltpu.VMEM(tables.shape, jnp.bfloat16),
            pltpu.VMEM(probe.shape, jnp.float32),
            pltpu.VMEM(msgs.shape, jnp.bfloat16),
            pltpu.VMEM(whole.shape, jnp.float32),
            pltpu.VMEM((8, LANES), jnp.int32),
            pltpu.SMEM((8, LANES), jnp.int32),
            pltpu.SMEM((kinds * CAP + BATCH,), jnp.int32),
            pltpu.SemaphoreType.DMA((6,)),
        ],
        MAIN_BYTES,
    )(tables, probe, msgs, ext)

    corner_two, line_one = swap(corner_two, row_two), swap(line_one, row_one)
    mid_one, mid_two = swap(mid_one, col_one), swap(mid_two, col_two)
    edge_two = swap(edge_two, row_two)
    end_one, end_two = kernel(
        functools.partial(sides_kernel, ncols, nrows), 3, [bf16((2, 2 * border, LANES))] * 2, "sides", cost=pl.CostEstimate(flops=10**10, bytes_accessed=10**6, transcendentals=0)
    )(grad, line_one, corner_two)
    end_one, end_two = swap(end_one, col_one), swap(end_two, col_two)
    whole_shape = f32((4, rows, cols))
    (out,) = kernel(
        functools.partial(middle_kernel, ncols),
        3,
        [whole_shape],
        "middle",
        [pltpu.VMEM((4, rows - 2 * border, cols), jnp.float32), pltpu.SemaphoreType.DMA((4,))],
        to=anywhere,
    )(grad, mid_one, mid_two)
    (out,) = kernel(
        functools.partial(final_kernel, ncols, nrows),
        [vmem] * 5 + [anywhere],
        [whole_shape],
        "final",
        [pltpu.VMEM((4, 2 * border, cols), jnp.float32), pltpu.SemaphoreType.DMA((4, 2))],
        to=anywhere,
        alias={5: 0},
    )(grad, line_one, edge_two, end_one, end_two, out)
    return out.reshape(objects.shape)


def solution(mesh):
    placed = (
        P(None, None, "row", "col"),
        P(),
        P("row", "col", None, None, None),
        P("row", "col", None),
        P("row", "col", None),
        P("row", "col", None),
    )
    return jax.shard_map(
        functools.partial(local, mesh.shape["col"], mesh.shape["row"]),
        mesh=mesh,
        in_specs=placed,
        out_specs=P(None, None, "row", "col"),
        check_vma=False,
    )
```

```python
import functools
import math

import jax
import jax.numpy as jnp
import numpy as np
from jax import lax
from jax.experimental import pallas as pl
from jax.experimental.pallas import tpu as pltpu
from jax.sharding import PartitionSpec as P

FRESNEL = 24.0
REACH_OFFSETS = (-3, -2, -1, 1, 2, 3, 4)
CAP = 2
LANES = 128
NOTE = 16
FIELDS = 4
VMEM_BYTES = 40 * 1024 * 1024
FULL_BYTES = 60 * 1024 * 1024
MAIN_BYTES = 48 * 1024 * 1024
BATCH = 6
HEAVY = pl.CostEstimate(flops=10**12, bytes_accessed=10**9, transcendentals=10**9)


def make_tables(width):
    idx = np.arange(width)
    angle = (idx[:, None] * idx[None, :] % width).astype(np.float32) * np.float32(2.0 * math.pi / width)
    scale = np.float32(1.0 / math.sqrt(width))
    f_re = np.cos(angle) * scale
    f_im = -np.sin(angle) * scale
    centred = (idx + width // 2) % width - width // 2
    theta = (centred * centred).astype(np.float32) * np.float32(math.pi * FRESNEL / (width * width))
    d_re = np.cos(theta)
    d_im = -np.sin(theta)
    m_re = d_re[:, None] * f_re - d_im[:, None] * f_im
    m_im = d_re[:, None] * f_im + d_im[:, None] * f_re
    k_re = f_re @ m_re + f_im @ m_im
    k_im = f_re @ m_im - f_im @ m_re
    tables = []
    for re, im in ((k_re, k_im), (f_re, f_im)):
        tables.append(np.block([[re, -im], [im, re]]))
        tables.append(np.block([[re, im], [-im, re]]))
    return jnp.asarray(np.stack(tables).astype(jnp.bfloat16))


def row_partners(nrows, ncols, idle):
    first = [((r, c), (r ^ 1, c)) for r in range(nrows) for c in range(ncols)]
    second = []
    for r in range(nrows):
        other = ((r + 1) ^ 1) - 1
        for c in range(ncols):
            second.append(((r, c), (other, c) if 0 <= other < nrows else idle(r, c)))
    return first, second


def col_partners(nrows, ncols):
    first = [((r, c), (r, c ^ 1)) for r in range(nrows) for c in range(ncols)]
    second = []
    for c in range(ncols):
        other = ((c + 1) ^ 1) - 1
        for r in range(nrows):
            second.append(((r, c), (r, other) if 0 <= other < ncols else (r ^ 1, c)))
    return first, second


def meet(at, step, turn, size):
    odd = (at // 2 if step == 2 else at) % 2
    return (at + size + step * (1 - 2 * odd) * (1 - 2 * turn)) % size


def routes(ncols):
    paired = [
        functools.partial(lambda step, turn, at: meet(at, step, turn, ncols), step, turn)
        for step in (1, 2, 3)
        for turn in (0, 1)
    ]
    return paired + [lambda at: (at + 4) % ncols]


def sides(axis, size):
    at = lax.axis_index(axis)
    return at % 2 == 0, (at > 0) & (at < size - 1)


def join_right(even, odd, border):
    low = lax.broadcasted_iota(jnp.int32, (1, LANES), 1) < border
    return jnp.where(low, even, pltpu.roll(odd, border, 1))


def join_left(even, odd, border):
    low = lax.broadcasted_iota(jnp.int32, (1, LANES), 1) < border
    return jnp.where(low, pltpu.roll(even, border, 1), odd)


def pack_kernel(ways, ncols, amps, owners, at_rows, at_cols, obj, *refs):
    side_one, side_two, msgs, tile, packed, held, chosen, ints, sem, sent = refs
    count, width = amps.shape[2:4]
    rows, cols = obj.shape[2:]
    border = width // 2
    small = [
        pltpu.make_async_copy(ref, ints.at[number], sem.at[number])
        for number, ref in enumerate((owners, at_rows, at_cols))
    ]
    tiles = [pltpu.make_async_copy(obj.at[pair], tile.at[pair], sem.at[3 + pair]) for pair in range(2)]
    patterns = pltpu.make_async_copy(amps.at[0, 0], held, sem.at[5])
    for copy in small + [patterns] + tiles:
        copy.start()
    for copy in small + [patterns]:
        copy.wait()

    myself = lax.axis_index("col")
    lane_id = lax.broadcasted_iota(jnp.int32, (NOTE, LANES), 1)
    copies = []
    for kind, way in enumerate(ways):
        owner = way(myself)
        found = jnp.int32(0)
        slots = [jnp.int32(0)] * CAP
        for j in range(count):
            mine = ints[0, 0, 0, j] == owner
            for slot in range(CAP):
                slots[slot] = jnp.where(mine & (found == slot), j, slots[slot])
            found = found + mine.astype(jnp.int32)
        note = jnp.zeros((NOTE, LANES), jnp.float32)
        for slot in range(CAP):
            j = slots[slot]
            chosen[kind, slot * width : (slot + 1) * width] = held[j]
            live = (found > slot).astype(jnp.int32)
            for field, value in enumerate((ints[1, 0, 0, j], ints[2, 0, 0, j], live)):
                here = lane_id == slot * FIELDS + field
                note = jnp.where(here, value.astype(jnp.float32), note)
        chosen[kind, CAP * width :] = note.astype(jnp.bfloat16)
        copies.append(pltpu.make_async_copy(chosen.at[kind], msgs.at[kind], sent.at[kind]))
        copies[-1].start()

    even_col, _ = sides("col", ncols)
    for pair in range(2):
        tiles[pair].wait()
        planes = (tile.at[pair, 0], tile.at[pair, 1])
        left = join_right(*(plane[:, :LANES] for plane in planes), border)
        right = join_left(*(plane[:, cols - LANES :] for plane in planes), border)
        packed[0, pair] = jnp.where(even_col, right, left).astype(jnp.bfloat16)
        packed[1, pair] = jnp.where(even_col, left, right).astype(jnp.bfloat16)
        for number, side in enumerate((side_one, side_two)):
            at = sem.at[6 + 2 * pair + number]
            copies.append(pltpu.make_async_copy(packed.at[number, pair], side.at[pair], at))
            copies[-1].start()
    for copy in copies:
        copy.wait()


def rows_kernel(ncols, nrows, came_one, came_two, obj, side, row_one, row_two):
    rows = side.shape[1]
    border = row_two.shape[2]
    blocks = row_two.shape[1] - 1
    even_col, inner = sides("col", ncols)
    even_row, _ = sides("row", nrows)
    for pair in range(2):
        one = came_one[pair].astype(jnp.float32)
        two = jnp.where(inner, came_two[pair].astype(jnp.float32), 0.0)
        near = jnp.where(even_col, one, two)
        far = jnp.where(even_col, two, one)
        side[2 * pair] = join_right(near, far, border).astype(jnp.bfloat16)
        side[2 * pair + 1] = join_left(near, far, border).astype(jnp.bfloat16)
    low = pl.multiple_of(jnp.where(even_row, rows - border, 0), border)
    high = pl.multiple_of(jnp.where(even_row, 0, rows - border), border)
    for message, start in ((row_one, low), (row_two, high)):
        for plane in range(4):
            for block in range(blocks):
                here = obj[plane, pl.ds(start, border), block * LANES : (block + 1) * LANES]
                message[plane, block] = here.astype(jnp.bfloat16)
            message[plane, blocks] = side[plane, pl.ds(start, border), :]


def matmul(first, second):
    return jnp.dot(first, second, preferred_element_type=jnp.float32)


def each_times(fields, table):
    size = fields[0].shape[0]
    whole = matmul(jnp.concatenate(fields, axis=0), table)
    return [whole[at : at + size] for at in range(0, whole.shape[0], size)]


def quarters(field):
    half = field.shape[0] // 2
    return field[:half, :half], field[:half, half:], field[half:, :half], field[half:, half:]


def joined(a, b, c, d):
    return jnp.concatenate(
        [jnp.concatenate([a, b], axis=1), jnp.concatenate([c, d], axis=1)], axis=0
    ).astype(jnp.bfloat16)


def swapped(field):
    a, b, c, d = quarters(field)
    return joined(a, c, b, d)


def after_rows(nrows, rows, border):
    even_row, inner = sides("row", nrows)
    one = pl.multiple_of(jnp.where(even_row, border + rows, 0), border)
    two = pl.multiple_of(jnp.where(even_row, 0, border + rows), border)
    return one, two, inner


def extend_kernel(nrows, obj, side, row_one, row_two, ext):
    rows, cols = obj.shape[1:]
    border = row_one.shape[2]
    blocks = cols // LANES
    after_one, after_two, inner = after_rows(nrows, rows, border)
    for plane in range(4):
        for block in range(blocks):
            ext[plane, block, border : border + rows] = obj[plane, :, block * LANES : (block + 1) * LANES]
        ext[plane, blocks, border : border + rows] = side[plane].astype(jnp.float32)
        for block in range(blocks + 1):
            ext[plane, block, pl.ds(after_one, border), :] = row_one[plane, block].astype(jnp.float32)
            ext[plane, block, pl.ds(after_two, border), :] = jnp.where(
                inner, row_two[plane, block].astype(jnp.float32), 0.0
            )


def main_kernel(batch, nrows, *refs):
    (given_tables, given_probe, given_msgs, given_ext), refs = refs[:4], refs[4:]
    (grad, out_one, out_two, corner_two), refs = refs[:4], refs[4:]
    tables, probe, msgs, ext, notes, notes_s, order, sem = refs
    kinds = msgs.shape[0]
    width = probe.shape[2]
    border = width // 2
    blocks = ext.shape[1] - 1
    rows = ext.shape[2] - 2 * border
    span = (blocks + 1) * LANES

    copies = [
        pltpu.make_async_copy(
            given_msgs.at[:, pl.ds(CAP * width, NOTE)], msgs.at[:, pl.ds(CAP * width, NOTE)], sem.at[0]
        ),
        pltpu.make_async_copy(given_ext, ext, sem.at[5]),
        pltpu.make_async_copy(given_tables, tables, sem.at[1]),
        pltpu.make_async_copy(given_probe, probe, sem.at[2]),
        pltpu.make_async_copy(
            given_msgs.at[:, pl.ds(0, CAP * width)], msgs.at[:, pl.ds(0, CAP * width)], sem.at[3]
        ),
    ]
    for copy in copies:
        copy.start()
    grad[...] = jnp.zeros_like(grad)
    copies[0].wait()
    for kind in range(kinds):
        note = msgs[kind, CAP * width :].astype(jnp.float32).astype(jnp.int32)
        notes[kind : kind + 1] = note[:1]
    copy = pltpu.make_async_copy(notes, notes_s, sem.at[4])
    copy.start()
    copy.wait()
    total = jnp.int32(0)
    for kind in range(kinds):
        for slot in range(CAP):
            order[total] = kind * CAP + slot
            total = total + notes_s[kind, slot * FIELDS + 2]
    for spare in range(batch):
        order[total + spare] = 0

    lane = lax.broadcasted_iota(jnp.int32, (1, LANES), 1)

    def stages(items):
        places = []
        for number in items:
            kind, slot = order[number] // CAP, order[number] % CAP
            row = notes_s[kind, slot * FIELDS]
            col = notes_s[kind, slot * FIELDS + 1]
            start = col + (span - border)
            start = jnp.where(start >= span, start - span, start)
            first = start // LANES
            shift = start % LANES
            second = jnp.where(first == blocks, 0, first + 1)
            places.append((kind, slot, row, first, second, shift))
        windows = []
        for _, _, row, first, second, shift in places:
            window = []
            for plane in range(4):
                a = ext[plane, first, pl.ds(row, width), :]
                b = ext[plane, second, pl.ds(row, width), :]
                both = jnp.where(lane >= shift, a, b)
                window.append(pltpu.roll(both, (LANES - shift) % LANES, 1))
            windows.append(window)
        fields = []
        for window in windows:
            parts = []
            for mode in range(2):
                p_re, p_im = probe[mode, 0], probe[mode, 1]
                parts.append((p_re * window[0] - p_im * window[1], p_re * window[1] + p_im * window[0]))
            fields.append(joined(parts[0][0], parts[1][0], parts[0][1], parts[1][1]))
        fields = [swapped(matmul(tables[0], f)) for f in fields]
        phis = each_times(fields, tables[1])
        fields = []
        for window, phi in zip(windows, phis):
            a_re, a_im, b_re, b_im = quarters(phi)
            w_re, w_im = window[2], window[3]
            fields.append(
                joined(
                    a_re * w_re - a_im * w_im,
                    b_re * w_re - b_im * w_im,
                    a_re * w_im + a_im * w_re,
                    b_re * w_im + b_im * w_re,
                )
            )
        fields = [swapped(matmul(tables[2], f)) for f in fields]
        fars = each_times(fields, tables[3])
        fields = []
        for place, far in zip(places, fars):
            a_re, a_im, b_re, b_im = quarters(far)
            inten = a_re * a_re + a_im * a_im + b_re * b_re + b_im * b_im
            kind, slot = place[:2]
            amp = msgs[kind, pl.ds(pl.multiple_of(slot * width, width), width), :].astype(jnp.float32)
            keep = 1.0 - amp * lax.rsqrt(jnp.maximum(inten, 1.0))
            fields.append(joined(a_re * keep, b_re * keep, a_im * keep, b_im * keep))
        fields = [swapped(matmul(tables[3], f)) for f in fields]
        seconds = each_times(fields, tables[2])
        fields = []
        for window, second in zip(windows, seconds):
            a_re, a_im, b_re, b_im = quarters(second)
            w_re, w_im = window[2], window[3]
            fields.append(
                joined(
                    w_re * a_re + w_im * a_im,
                    w_re * b_re + w_im * b_im,
                    w_re * a_im - w_im * a_re,
                    w_re * b_im - w_im * b_re,
                )
            )
        fields = [swapped(matmul(tables[1], f)) for f in fields]
        firsts = each_times(fields, tables[0])
        for number, place, phi, one, two in zip(items, places, phis, firsts, seconds):
            _, _, row, first, second, shift = place
            sums = []
            probes = (probe[0, 0], probe[0, 1], probe[1, 0], probe[1, 1])
            for left, right in ((probes, one), (quarters(phi), two)):
                p_re, p_im, q_re, q_im = left
                a_re, a_im, b_re, b_im = quarters(right)
                sums.append(p_re * a_re + p_im * a_im + q_re * b_re + q_im * b_im)
                sums.append(p_re * a_im - p_im * a_re + q_re * b_im - q_im * b_re)
            live = number < total
            for plane in range(4):
                moved = pltpu.roll(sums[plane], shift, 1)
                grad[plane, first, pl.ds(row, width), :] += jnp.where((lane >= shift) & live, moved, 0.0)
                grad[plane, second, pl.ds(row, width), :] += jnp.where((lane < shift) & live, moved, 0.0)

    def visit(step, carry):
        stages([batch * step + item for item in range(batch)])
        return carry

    for copy in copies[1:]:
        copy.wait()
    lax.fori_loop(0, (total + batch - 1) // batch, visit, 0)

    after_one, after_two, _ = after_rows(nrows, rows, border)
    for plane in range(4):
        for block in range(blocks + 1):
            out_one[plane, block] = grad[plane, block, pl.ds(after_one, border), :].astype(jnp.bfloat16)
            two = grad[plane, block, pl.ds(after_two, border), :].astype(jnp.bfloat16)
            if block < blocks:
                out_two[plane, block] = two
            else:
                corner_two[plane] = two


def pack_sides(ncols, even, odd, border):
    even_col, _ = sides("col", ncols)
    right, left = join_right(even, odd, border), join_left(even, odd, border)
    return jnp.where(even_col, right, left).astype(jnp.bfloat16), jnp.where(even_col, left, right).astype(jnp.bfloat16)


def row_parts(nrows, rows, border):
    even_row, inner = sides("row", nrows)
    most = pl.multiple_of(jnp.where(even_row, border, 0), border)
    rest = pl.multiple_of(jnp.where(even_row, 0, rows - border), border)
    return even_row, inner, most, rest


def with_rows(even_row, region, came):
    border = came.shape[0]
    came = came.astype(jnp.float32)
    top = region[:border] + jnp.where(even_row, 0.0, came)
    bottom = region[-border:] + jnp.where(even_row, came, 0.0)
    return jnp.concatenate([top, region[border:-border], bottom], axis=0)


def most_kernel(ncols, nrows, grad, row_one, side_one, side_two):
    blocks = row_one.shape[1] - 1
    border = row_one.shape[2]
    rows = grad.shape[2] - 2 * border
    height = rows - border
    even_row, _, most, _ = row_parts(nrows, rows, border)
    for pair in range(2):
        even, odd = (
            with_rows(even_row, grad[plane, blocks, pl.ds(border + most, height), :], row_one[plane, blocks])
            for plane in (2 * pair, 2 * pair + 1)
        )
        side_one[pair], side_two[pair] = pack_sides(ncols, even, odd, border)


def sides_kernel(ncols, nrows, grad, corner_two, side_one, side_two):
    blocks = grad.shape[1] - 1
    border = corner_two.shape[1]
    rows = grad.shape[2] - 2 * border
    _, inner, _, rest = row_parts(nrows, rows, border)
    for pair in range(2):
        even, odd = (
            grad[plane, blocks, pl.ds(border + rest, border), :]
            + jnp.where(inner, corner_two[plane].astype(jnp.float32), 0.0)
            for plane in (2 * pair, 2 * pair + 1)
        )
        side_one[pair], side_two[pair] = pack_sides(ncols, even, odd, border)


def column_sums(ncols, border, came_one, came_two, pair):
    low = lax.broadcasted_iota(jnp.int32, (1, LANES), 1) < border
    even_col, inner = sides("col", ncols)
    one = came_one[pair].astype(jnp.float32)
    two = jnp.where(inner, came_two[pair].astype(jnp.float32), 0.0)
    near, far = jnp.where(even_col, two, one), jnp.where(even_col, one, two)
    return (
        (jnp.where(low, near, 0.0), jnp.where(low, 0.0, pltpu.roll(far, border, 1))),
        (jnp.where(low, pltpu.roll(near, border, 1), 0.0), jnp.where(low, 0.0, far)),
    )


def middle_kernel(ncols, nrows, grad, row_one, mid_one, mid_two, out, whole, sem):
    height, cols = whole.shape[1:]
    rows = out.shape[1]
    border = rows - height
    blocks = cols // LANES
    even_row, _, most, _ = row_parts(nrows, rows, border)
    copies = []
    for pair in range(2):
        for odd, (first, last) in enumerate(column_sums(ncols, border, mid_one, mid_two, pair)):
            plane = 2 * pair + odd
            for block in range(blocks):
                total = with_rows(
                    even_row, grad[plane, block, pl.ds(border + most, height), :], row_one[plane, block]
                )
                if block == 0:
                    total = total + first
                if block == blocks - 1:
                    total = total + last
                whole[plane, :, block * LANES : (block + 1) * LANES] = total
            span = pl.ds(most, height)
            copies.append(pltpu.make_async_copy(whole.at[plane], out.at[plane, span], sem.at[plane]))
            copies[-1].start()
    return copies


def rest_kernel(ncols, nrows, grad, row_two, end_one, end_two, out, whole, sem):
    blocks, border = row_two.shape[1:3]
    rows = grad.shape[2] - 2 * border
    _, inner, _, rest = row_parts(nrows, rows, border)
    copies = []
    for pair in range(2):
        for odd, (first, last) in enumerate(column_sums(ncols, border, end_one, end_two, pair)):
            plane = 2 * pair + odd
            for block in range(blocks):
                total = grad[plane, block, pl.ds(border + rest, border), :]
                total = total + jnp.where(inner, row_two[plane, block].astype(jnp.float32), 0.0)
                if block == 0:
                    total = total + first
                if block == blocks - 1:
                    total = total + last
                whole[plane, :, block * LANES : (block + 1) * LANES] = total
            span = pl.ds(rest, border)
            copies.append(pltpu.make_async_copy(whole.at[plane], out.at[plane, span], sem.at[plane]))
            copies[-1].start()
    return copies


def final_kernel(ncols, nrows, grad, row_one, row_two, mid_one, mid_two, end_one, end_two, out, *refs):
    most, rest, most_sem, rest_sem = refs
    copies = middle_kernel(ncols, nrows, grad, row_one, mid_one, mid_two, out, most, most_sem)
    copies += rest_kernel(ncols, nrows, grad, row_two, end_one, end_two, out, rest, rest_sem)
    for copy in copies:
        copy.wait()


def local(ncols, nrows, objects, probe, amplitudes, owners, off_rows, off_cols):
    width = amplitudes.shape[-1]
    border = width // 2
    count = amplitudes.shape[2]
    rows, cols = objects.shape[2:]
    blocks = cols // LANES
    obj = objects.reshape(4, rows, cols)
    vmem = pl.BlockSpec(memory_space=pltpu.VMEM)
    anywhere = pl.BlockSpec(memory_space=pl.ANY)
    bf16 = functools.partial(jax.ShapeDtypeStruct, dtype=jnp.bfloat16)
    f32 = functools.partial(jax.ShapeDtypeStruct, dtype=jnp.float32)

    def kernel(body, ins, outs, name, scratch=(), limit=VMEM_BYTES, cost=None, to=vmem, alias={}):
        return pl.pallas_call(
            body,
            out_shape=outs,
            in_specs=ins if isinstance(ins, list) else [vmem] * ins,
            out_specs=[to] * len(outs),
            scratch_shapes=list(scratch),
            compiler_params=pltpu.CompilerParams(vmem_limit_bytes=limit),
            cost_estimate=cost,
            input_output_aliases=alias,
            name=name,
        )

    def across(array, way):
        return lax.ppermute(array, "col", [(i, way(i)) for i in range(ncols)])

    def swap(array, pairs):
        flat = [(a * ncols + b, c * ncols + d) for (a, b), (c, d) in pairs]
        return lax.ppermute(array, ("row", "col"), flat)

    row_one, row_two = row_partners(nrows, ncols, lambda r, c: (nrows - 1 - r, c))
    col_one, col_two = col_partners(nrows, ncols)
    if ncols == 8:
        ways = [functools.partial(lambda to, at: to, to) for to in range(ncols)]
    else:
        ways = routes(ncols)
    kinds = len(ways)
    line_shape = bf16((4, blocks + 1, border, LANES))
    side_shape = bf16((2, rows, LANES))

    side_one, side_two, msgs = kernel(
        functools.partial(pack_kernel, ways, ncols),
        [anywhere] * 5,
        [side_shape] * 2 + [bf16((kinds, CAP * width + NOTE, LANES))],
        "pack",
        [
            pltpu.VMEM(objects.shape, jnp.float32),
            pltpu.VMEM((2,) + side_shape.shape, jnp.bfloat16),
            pltpu.VMEM((count, width, width), jnp.bfloat16),
            pltpu.VMEM((kinds, CAP * width + NOTE, LANES), jnp.bfloat16),
            pltpu.SMEM((3,) + owners.shape, jnp.int32),
            pltpu.SemaphoreType.DMA((10,)),
            pltpu.SemaphoreType.DMA((kinds,)),
        ],
        FULL_BYTES,
        to=anywhere,
    )(amplitudes, owners, off_rows, off_cols, objects)
    came_one, came_two = swap(side_one, col_one), swap(side_two, col_two)
    if ncols == 8:
        msgs = lax.all_to_all(msgs, "col", 0, 0)
    else:
        msgs = jnp.stack([across(msgs[kind], way) for kind, way in enumerate(ways)])
    side, line_one, line_two = kernel(
        functools.partial(rows_kernel, ncols, nrows),
        3,
        [bf16((4, rows, LANES))] + [line_shape] * 2,
        "rows",
        cost=HEAVY,
    )(came_one, came_two, obj)
    line_one, line_two = swap(line_one, row_one), swap(line_two, row_two)

    whole = f32((4, blocks + 1, rows + 2 * border, LANES))
    (ext,) = kernel(functools.partial(extend_kernel, nrows), 4, [whole], "extend")(
        obj, side, line_one, line_two
    )
    tables = make_tables(width)
    edge_shape = bf16((4, blocks, border, LANES))
    corner_shape = bf16((4, border, LANES))
    grad, line_one, edge_two, corner_two = kernel(
        functools.partial(main_kernel, BATCH, nrows),
        [anywhere] * 4,
        [whole, line_shape, edge_shape, corner_shape],
        "gradients",
        [
            pltpu.VMEM(tables.shape, jnp.bfloat16),
            pltpu.VMEM(probe.shape, jnp.float32),
            pltpu.VMEM(msgs.shape, jnp.bfloat16),
            pltpu.VMEM(whole.shape, jnp.float32),
            pltpu.VMEM((8, LANES), jnp.int32),
            pltpu.SMEM((8, LANES), jnp.int32),
            pltpu.SMEM((kinds * CAP + BATCH,), jnp.int32),
            pltpu.SemaphoreType.DMA((6,)),
        ],
        MAIN_BYTES,
    )(tables, probe, msgs, ext)

    line_one, corner_two = swap(line_one, row_one), swap(corner_two, row_two)
    mid_one, mid_two = kernel(
        functools.partial(most_kernel, ncols, nrows), 2, [bf16((2, rows - border, LANES))] * 2, "most"
    )(grad, line_one)
    mid_one, mid_two, edge_two = lax.optimization_barrier((mid_one, mid_two, edge_two))
    mid_one, mid_two = swap(mid_one, col_one), swap(mid_two, col_two)
    edge_two = swap(edge_two, row_two)
    end_one, end_two = kernel(
        functools.partial(sides_kernel, ncols, nrows),
        2,
        [bf16((2, border, LANES))] * 2,
        "sides",
        cost=pl.CostEstimate(flops=10**10, bytes_accessed=10**6, transcendentals=0),
    )(grad, corner_two)
    end_one, end_two = swap(end_one, col_one), swap(end_two, col_two)
    (out,) = kernel(
        functools.partial(final_kernel, ncols, nrows),
        7,
        [f32((4, rows, cols))],
        "final",
        [
            pltpu.VMEM((4, rows - border, cols), jnp.float32),
            pltpu.VMEM((4, border, cols), jnp.float32),
            pltpu.SemaphoreType.DMA((4,)),
            pltpu.SemaphoreType.DMA((4,)),
        ],
        to=anywhere,
    )(grad, line_one, edge_two, mid_one, mid_two, end_one, end_two)
    return out.reshape(objects.shape)


def solution(mesh):
    placed = (
        P(None, None, "row", "col"),
        P(),
        P("row", "col", None, None, None),
        P("row", "col", None),
        P("row", "col", None),
        P("row", "col", None),
    )
    return jax.shard_map(
        functools.partial(local, mesh.shape["col"], mesh.shape["row"]),
        mesh=mesh,
        in_specs=placed,
        out_specs=P(None, None, "row", "col"),
        check_vma=False,
    )
```
